32 devices in a mesh: row: 4 (over z), col: 8 (over y, x, core).
Axes of the slice: x: 2, y: 2, z: 4, core: 2. Of those that a mesh axis runs over, the one named last changes fastest.
Arguments:
- points: float32 [64, 4096], P(None, ('row', 'col')), may hold values from -6 to 6
- targets: float32 [4096], P(('row', 'col')), may hold values from -6 to 6
- probes: float32 [32, 4096], P(None, ('row', 'col')), may hold values from -6 to 6
- lengthscale: float32 [1], replicated, may hold values from 3.5 to 5
- outputscale: float32 [1], replicated, may hold values from 0.5 to 2
- noise: float32 [1], replicated, may hold values from 0.05 to 0.5
Outputs:
- solution: float32 [33, 4096], P(None, ('row', 'col'))
- residual: float32 [33, 4096], P(None, ('row', 'col'))
- direction: float32 [33, 4096], P(None, ('row', 'col'))
- length_products: float32 [32, 4096], P(None, ('row', 'col'))
- scale_products: float32 [32, 4096], P(None, ('row', 'col'))
The draws below stay inside these ranges and needn't reach their ends.
All inputs are finite; a program needn't handle non-finite values.
Results may differ from the reference program's by a relative error of at most 0.0003.
Values sent between devices are 32-bit elements; how exact they have to be, the bound alone decides.
A program may use at most 64 MiB of HBM per device.

```python
import math
import jax
import jax.numpy as jnp
from jax import lax

F = 64
PROBES = 32
N = 4096


def level_of(stream_key, extent, split, low, high):
    factor_of, own = 1.0, jax.random.fold_in(stream_key, 6)
    for position, shards_of in split:
        draws = jnp.exp(jax.random.uniform(jax.random.fold_in(own, position), (shards_of,), jnp.float32, low / len(split), high / len(split)))
        factor_of = factor_of * jnp.repeat(draws, extent[position] // shards_of).reshape([-1 if axis == position else 1 for axis in range(len(extent))])
    return factor_of


def scatter_about(own_key, extent, width, bound, pieces=(), kind=jnp.bfloat16):
    loudness = level_of(own_key, extent, pieces, -0.22, 0.18) if pieces else 1.0
    drawn = jax.random.normal(own_key, extent, jnp.float32) * width * loudness
    return jnp.minimum(jnp.maximum(drawn, -bound), bound).astype(kind)


def setup_inputs(seed: int = 0) -> dict:
    key_list = jax.random.split(jax.random.key(seed), 7)
    return {
        "points": scatter_about(key_list[0], (F, N), 1.0, 6.0, ((1, 32),), jnp.float32),
        "targets": scatter_about(key_list[1], (N,), 1.0, 6.0, ((0, 32),), jnp.float32),
        "probes": scatter_about(key_list[2], (PROBES, N), 1.0, 6.0, ((1, 32),), jnp.float32),
        "lengthscale": jnp.clip(jnp.exp(jax.random.uniform(key_list[3], (1,), jnp.float32, math.log(3.5), math.log(5.0))), 3.5, 5.0),
        "outputscale": jnp.clip(jnp.exp(jax.random.uniform(key_list[4], (1,), jnp.float32, math.log(0.5), math.log(2.0))), 0.5, 2.0),
        "noise": jnp.clip(jnp.exp(jax.random.uniform(key_list[5], (1,), jnp.float32, math.log(0.05), math.log(0.5))), 0.05, 0.5),
    }


def reference(points, targets, probes, lengthscale, outputscale, noise):
    rhs = jnp.concatenate([targets[None, :], probes], 0)
    inv_two = 0.5 / (lengthscale[0] * lengthscale[0])
    total = points.shape[1]
    sq_all = jnp.sum(points * points, axis=0)
    block_rows = math.gcd(total, 256)
    count = total // block_rows

    def one_block(index):
        start = (index * block_rows).astype(jnp.int32)
        x_rows = lax.dynamic_slice_in_dim(points, start, block_rows, 1)
        sq_rows = lax.dynamic_slice_in_dim(sq_all, start, block_rows, 0)
        dots = lax.dot_general(points, x_rows, (((0,), (0,)), ((), ())), precision=lax.Precision.HIGHEST, preferred_element_type=jnp.float32)
        dist = jnp.maximum(sq_all[:, None] + sq_rows[None, :] - 2.0 * dots, 0.0)
        kern = jnp.exp(-dist * inv_two)
        eb_part = jnp.dot(rhs, kern, precision=lax.Precision.HIGHEST, preferred_element_type=jnp.float32)
        ed_part = jnp.dot(probes, kern * dist, precision=lax.Precision.HIGHEST, preferred_element_type=jnp.float32)
        return eb_part, ed_part

    eb_blocks, ed_blocks = lax.map(one_block, jnp.arange(count, dtype=jnp.int32))
    eb = jnp.transpose(eb_blocks, (1, 0, 2)).reshape(rhs.shape[0], total)
    ed = jnp.transpose(ed_blocks, (1, 0, 2)).reshape(probes.shape[0], total)
    scale = outputscale[0]
    kb = scale * eb + noise[0] * rhs
    scale_products = eb[1:]
    length_products = scale / (lengthscale[0] ** 3) * ed
    norm_old = jnp.sum(rhs * rhs, axis=1)
    curv = jnp.sum(rhs * kb, axis=1)
    alpha = norm_old / curv
    solution = alpha[:, None] * rhs
    residual = rhs - alpha[:, None] * kb
    norm_new = jnp.sum(residual * residual, axis=1)
    direction = residual + (norm_new / norm_old)[:, None] * rhs
    return solution, residual, direction, length_products, scale_products
```

```python
import functools

import jax
import jax.numpy as jnp
from jax import lax
from jax.experimental import pallas as pl
from jax.experimental.pallas import tpu as pltpu
from jax.sharding import PartitionSpec as P

MESH = pl.DeviceIdType.MESH
F32 = jnp.float32
BF16 = jnp.bfloat16
NT = (((1,), (1,)), ((), ()))


def up_to(value, multiple):
    return (value + multiple - 1) // multiple * multiple


def split_three(value):
    high = value.astype(BF16)
    rest = value - high.astype(F32)
    middle = rest.astype(BF16)
    low = (rest - middle.astype(F32)).astype(BF16)
    return high, middle, low


def kernel(
    n_row,
    n_quad,
    feats,
    n_probes,
    x_ref,
    t_ref,
    p_ref,
    ls_ref,
    os_ref,
    no_ref,
    sol_ref,
    res_ref,
    dir_ref,
    len_ref,
    scl_ref,
    held,
    mate_block,
    own_split,
    own_sq,
    acc,
    part_out,
    part_in,
    sums,
    recv_sem,
    up_sem,
    down_sem,
    side_sem,
    mate_send,
    mate_recv,
    sum_send,
    sum_recv,
):
    r = lax.axis_index("row")
    col = lax.axis_index("col")
    q = col // 2
    core = col % 2
    n_peers = n_row * n_quad
    me = r * n_quad + q
    width = x_ref.shape[1]
    rhs_rows = up_to(n_probes + 1, 8)
    lhs_rows = up_to(n_probes + 1, 16)
    mate = {"row": r, "col": q * 2 + (1 - core)}

    def device(row, quad):
        return {"row": row, "col": quad * 2 + core}

    barrier = pltpu.get_barrier_semaphore()
    pl.semaphore_signal(barrier, inc=1, device_id=mate, device_id_type=MESH)

    @pl.loop(1, n_peers)
    def _(k):
        peer = (me + k) % n_peers
        pl.semaphore_signal(
            barrier, inc=1, device_id=device(peer // n_quad, peer % n_quad), device_id_type=MESH
        )

    mine = held.at[r, q]
    mine[0:feats, :] = x_ref[...]
    mine[feats : feats + n_probes, :] = p_ref[...]
    mine[feats + n_probes :, :] = jnp.concatenate(
        [t_ref[...], jnp.zeros((rhs_rows - n_probes - 1, width), F32)], 0
    )
    acc[...] = jnp.zeros_like(acc)
    pl.semaphore_wait(barrier, n_peers)

    def copy(src, dst, send, recv, target):
        return pltpu.make_async_remote_copy(
            src_ref=src, dst_ref=dst, send_sem=send, recv_sem=recv, device_id=target, device_id_type=MESH
        )

    def pass_on(row, quad, send, to_row, to_quad):
        slot = held.at[row, quad]
        return copy(slot, slot, send, recv_sem.at[row, quad], device(to_row, to_quad))

    def arrived(row, quad):
        slot = held.at[row, quad]
        copy(slot, slot, mate_send.at[0], recv_sem.at[row, quad], mate).wait_recv()

    paired = jnp.minimum(r, n_row - 1 - r)
    low_side = (2 * r < n_row).astype(jnp.int32)

    def order(t):
        near = r + (t % 2) * (-((t + 1) // 2)) + (1 - t % 2) * (t // 2)
        far = low_side * t + (1 - low_side) * (n_row - 1 - t)
        inside = (t <= 2 * paired).astype(jnp.int32)
        return inside * near + (1 - inside) * far

    def up(row):
        return pass_on(row, q, up_sem.at[row], jnp.minimum(r + 1, n_row - 1), q)

    def down(row):
        return pass_on(row, q, down_sem.at[row], jnp.maximum(r - 1, 0), q)

    def goes_up(row):
        return jnp.logical_and(row <= r, r + 1 < n_row)

    def goes_down(row):
        return jnp.logical_and(row >= r, r >= 1)

    square = n_quad == 4
    near_x = (q // 2) * 2 + (1 - q % 2)
    near_y = (1 - q // 2) * 2 + q % 2
    across = 3 - q

    def side(row, k):
        if square:
            if k == 0:
                return pass_on(row, q, side_sem.at[row, 0], r, near_x)
            if k == 1:
                return pass_on(row, q, side_sem.at[row, 1], r, near_y)
            even = 1 - row % 2
            source = even * near_x + (1 - even) * near_y
            target = even * near_y + (1 - even) * near_x
            return pass_on(row, source, side_sem.at[row, 2], r, target)
        return pass_on(row, q, side_sem.at[row, k], r, (q + k + 1) % n_quad)

    def spread(row):
        @pl.when(goes_up(row))
        def _():
            up(row).start()

        @pl.when(goes_down(row))
        def _():
            down(row).start()

        if square:
            side(row, 0).start()
            side(row, 1).start()
        else:

            @pl.loop(0, n_quad - 1)
            def _(k):
                side(row, k).start()

    to_mate = copy(mine, mate_block, mate_send.at[0], mate_recv.at[0], mate)
    to_mate.start()
    spread(r)

    inv_two = 0.5 / (ls_ref[0] * ls_ref[0])

    def prepare(half, block):
        x = jnp.transpose(block[0:feats, :])
        rows = pl.ds(half * width, width)
        own_sq[rows, :] = jnp.broadcast_to(jnp.sum(x * x, axis=1, keepdims=True), (width, width))
        high, middle, low = split_three(-2.0 * x)
        own_split[rows, :] = jnp.concatenate([high, high, middle, high, low, middle], 1)

    prepare(0, mine)
    to_mate.wait_recv()
    prepare(1, mate_block)

    def absorb(row, quad):
        block = held.at[row, quad]
        x = block[0:feats, :]
        high, middle, low = split_three(x)
        stack = jnp.concatenate([high, middle, high, low, high, middle], 0)
        dots = jnp.dot(own_split[...], stack, preferred_element_type=F32)
        sq = jnp.sum(x * x, axis=0, keepdims=True)
        dist = jnp.maximum((own_sq[...] + sq) + dots, 0.0)
        kern = jnp.exp(dist * (-inv_two))
        both = jnp.concatenate([kern, kern * dist], 0)
        both_high = both.astype(BF16)
        both_middle = (both - both_high.astype(F32)).astype(BF16)
        rhs = jnp.concatenate(
            [block[feats:, :], jnp.zeros((lhs_rows - rhs_rows, width), F32)], 0
        )
        b_high, b_middle, b_low = split_three(rhs)
        first = lax.dot_general(
            jnp.concatenate([b_high, b_middle, b_low], 0), both_high, NT, preferred_element_type=F32
        )
        second = lax.dot_general(
            jnp.concatenate([b_high, b_middle], 0), both_middle, NT, preferred_element_type=F32
        )
        small = (first[2 * lhs_rows :] + second[lhs_rows:]) + (first[lhs_rows : 2 * lhs_rows] + second[:lhs_rows])
        acc[...] += first[:lhs_rows] + small

    def others(row):
        if square:
            arrived(row, near_x)
            arrived(row, near_y)
            side(row, 2).start()
            absorb(row, near_x)
            absorb(row, near_y)
        else:

            @pl.loop(1, n_quad)
            def _(k):
                quad = (q + k) % n_quad
                arrived(row, quad)
                absorb(row, quad)

    def last(row):
        if square:
            arrived(row, across)
            absorb(row, across)

    for t in range(n_row + 2):
        if t < n_row:
            row = order(t)
            if t > 0:
                arrived(row, q)
                spread(row)
            absorb(row, q)
        if 1 <= t <= n_row:
            others(order(t - 1))
        if t >= 2:
            last(order(t - 2))

    part_out[0] = acc[0:rhs_rows, 0:width]
    part_out[1] = acc[0:rhs_rows, width : 2 * width]
    part_out[2] = acc[0:rhs_rows, 3 * width : 4 * width]
    swap = copy(part_out, part_in, mate_send.at[1], mate_recv.at[1], mate)
    swap.start()
    rhs = mine[feats:, :]
    rhs_mate = mate_block[feats:, :]
    scale = os_ref[0]
    noise = no_ref[0]
    norms = rhs * rhs + rhs_mate * rhs_mate
    swap.wait_recv()
    eb = part_out[0] + part_in[1]
    eb_mate = part_out[1] + part_in[0]
    ed = acc[0:rhs_rows, 2 * width : 3 * width] + part_in[2]
    kb = scale * eb + noise * rhs
    kb_mate = scale * eb_mate + noise * rhs_mate
    terms = [norms, rhs * kb + rhs_mate * kb_mate, kb * kb + kb_mate * kb_mate]
    lanes = up_to(3 * rhs_rows, 128)
    if lanes > 3 * rhs_rows:
        terms.append(jnp.zeros((lanes - 3 * rhs_rows, width), F32))
    row_sums = lax.dot_general(
        jnp.ones((8, width), F32),
        jnp.concatenate(terms, 0),
        NT,
        precision=lax.Precision.HIGHEST,
        preferred_element_type=F32,
    )
    sums[me] = row_sums[0:1]

    def share(k):
        peer = (me + k) % n_peers
        return copy(
            sums.at[me], sums.at[me], sum_send.at[peer], sum_recv.at[me],
            device(peer // n_quad, peer % n_quad),
        )

    @pl.loop(1, n_peers)
    def _(k):
        share(k).start()

    scl_ref[...] = eb[0:n_probes]
    len_ref[...] = (scale / (ls_ref[0] * ls_ref[0] * ls_ref[0])) * ed[0:n_probes]

    @pl.loop(1, n_peers)
    def _(k):
        peer = (me + k) % n_peers
        copy(sums.at[peer], sums.at[peer], mate_send.at[0], sum_recv.at[peer], mate).wait_recv()

    total = jnp.sum(sums[...], axis=0)
    lane = lax.broadcasted_iota(jnp.int32, (rhs_rows, lanes), 1)
    sub = lax.broadcasted_iota(jnp.int32, (rhs_rows, lanes), 0)

    def column(index):
        picked = jnp.where(lane == sub + index * rhs_rows, total, 0.0)
        return jnp.sum(picked, axis=1, keepdims=True)

    norm_old, curv, kb_sq = column(0), column(1), column(2)
    alpha = norm_old / curv
    norm_new = jnp.maximum(alpha * (alpha * kb_sq) - norm_old, 0.0)
    beta = norm_new / norm_old
    solved = alpha * rhs
    residual = rhs - alpha * kb
    direction = residual + beta * rhs
    for ref, value in ((sol_ref, solved), (res_ref, residual), (dir_ref, direction)):
        ref[0:1, :] = value[n_probes : n_probes + 1]
        ref[1 : n_probes + 1, :] = value[0:n_probes]

    to_mate.wait_send()
    swap.wait_send()

    @pl.loop(0, n_row)
    def _(row):
        @pl.when(goes_up(row))
        def _():
            up(row).wait_send()

        @pl.when(goes_down(row))
        def _():
            down(row).wait_send()

        if square:
            for k in range(3):
                side(row, k).wait_send()
        else:

            @pl.loop(0, n_quad - 1)
            def _(k):
                side(row, k).wait_send()

    @pl.loop(1, n_peers)
    def _(k):
        share(k).wait_send()


def shards(n_row, n_quad, points, targets, probes, lengthscale, outputscale, noise):
    feats, width = points.shape
    n_probes = probes.shape[0]
    n_peers = n_row * n_quad
    rhs_rows = up_to(n_probes + 1, 8)
    lhs_rows = up_to(n_probes + 1, 16)
    rows = feats + rhs_rows
    vmem = pl.BlockSpec(memory_space=pltpu.VMEM)
    smem = pl.BlockSpec(memory_space=pltpu.SMEM)
    tall = jax.ShapeDtypeStruct((n_probes + 1, width), F32)
    short = jax.ShapeDtypeStruct((n_probes, width), F32)
    return pl.pallas_call(
        functools.partial(kernel, n_row, n_quad, feats, n_probes),
        out_shape=(tall, tall, tall, short, short),
        in_specs=[vmem, vmem, vmem, smem, smem, smem],
        out_specs=(vmem,) * 5,
        scratch_shapes=[
            pltpu.VMEM((n_row, n_quad, rows, width), F32),
            pltpu.VMEM((rows, width), F32),
            pltpu.VMEM((2 * width, 6 * feats), BF16),
            pltpu.VMEM((2 * width, width), F32),
            pltpu.VMEM((lhs_rows, 4 * width), F32),
            pltpu.VMEM((3, rhs_rows, width), F32),
            pltpu.VMEM((3, rhs_rows, width), F32),
            pltpu.VMEM((n_peers, 1, up_to(3 * rhs_rows, 128)), F32),
            pltpu.SemaphoreType.DMA((n_row, n_quad)),
            pltpu.SemaphoreType.DMA((n_row,)),
            pltpu.SemaphoreType.DMA((n_row,)),
            pltpu.SemaphoreType.DMA((n_row, max(n_quad - 1, 3))),
            pltpu.SemaphoreType.DMA((2,)),
            pltpu.SemaphoreType.DMA((2,)),
            pltpu.SemaphoreType.DMA((n_peers,)),
            pltpu.SemaphoreType.DMA((n_peers,)),
        ],
        compiler_params=pltpu.CompilerParams(
            collective_id=0,
            has_side_effects=True,
            vmem_limit_bytes=n_peers * rows * width * 4 + (16 << 20),
        ),
    )(points, targets[None, :], probes, lengthscale, outputscale, noise)


def solution(mesh):
    split = ("row", "col")
    wide = P(None, split)
    return jax.shard_map(
        functools.partial(shards, mesh.shape["row"], mesh.shape["col"] // 2),
        mesh=mesh,
        in_specs=(wide, P(split), wide, P(), P(), P()),
        out_specs=(wide,) * 5,
        check_vma=False,
    )
```

```python
import functools

import jax
import jax.numpy as jnp
from jax import lax
from jax.experimental import pallas as pl
from jax.experimental.pallas import tpu as pltpu
from jax.sharding import PartitionSpec as P

MESH = pl.DeviceIdType.MESH
F32 = jnp.float32
BF16 = jnp.bfloat16
NT = (((1,), (1,)), ((), ()))


def up_to(value, multiple):
    return (value + multiple - 1) // multiple * multiple


def split_three(value):
    high = value.astype(BF16)
    rest = value - high.astype(F32)
    middle = rest.astype(BF16)
    low = (rest - middle.astype(F32)).astype(BF16)
    return high, middle, low


def kernel(
    n_row,
    n_col,
    feats,
    n_probes,
    x_hbm,
    t_hbm,
    p_hbm,
    ls_ref,
    os_ref,
    no_ref,
    sol_hbm,
    res_hbm,
    dir_hbm,
    len_hbm,
    scl_hbm,
    held,
    plane,
    targets,
    own_split,
    own_sq,
    acc,
    part_out,
    part_in,
    line_sums,
    plane_sums,
    load_sem,
    line_send,
    line_recv,
    plane_send,
    plane_recv,
    part_send,
    part_recv,
    ls_send,
    ls_recv,
    ps_send,
    ps_recv,
    tall_out,
    short_out,
    store_sem,
):
    r = lax.axis_index("row")
    col = lax.axis_index("col")
    n_quad = n_col // 2
    q = col // 2
    width = x_hbm.shape[1]
    rhs_rows = up_to(n_probes + 1, 8)
    lhs_rows = up_to(n_probes + 1, 16)

    mine = held.at[r]
    loads = [
        pltpu.make_async_copy(x_hbm, mine.at[0:feats], load_sem.at[0]),
        pltpu.make_async_copy(p_hbm, mine.at[feats : feats + n_probes], load_sem.at[1]),
        pltpu.make_async_copy(t_hbm, targets, load_sem.at[2]),
    ]
    for load in loads:
        load.start()

    barrier = pltpu.get_barrier_semaphore()

    def on_line(k):
        return (r + k) % n_row

    def on_plane(k):
        return (col + k) % n_col

    @pl.loop(1, n_row)
    def _(k):
        pl.semaphore_signal(
            barrier, inc=1, device_id={"row": on_line(k), "col": col}, device_id_type=MESH
        )

    @pl.loop(1, n_col)
    def _(k):
        pl.semaphore_signal(
            barrier, inc=1, device_id={"row": r, "col": on_plane(k)}, device_id_type=MESH
        )

    acc[...] = jnp.zeros_like(acc)
    for load in loads:
        load.wait()
    mine[feats + n_probes :, :] = jnp.concatenate(
        [targets[...], jnp.zeros((rhs_rows - n_probes - 1, width), F32)], 0
    )
    pl.semaphore_wait(barrier, n_row + n_col - 2)

    def copy(src, dst, send, recv, row, column):
        return pltpu.make_async_remote_copy(
            src_ref=src, dst_ref=dst, send_sem=send, recv_sem=recv,
            device_id={"row": row, "col": column}, device_id_type=MESH,
        )

    paired = jnp.minimum(r, n_row - 1 - r)
    low_side = (2 * r < n_row).astype(jnp.int32)

    def order(t):
        near = r + (t % 2) * (-((t + 1) // 2)) + (1 - t % 2) * (t // 2)
        far = low_side * t + (1 - low_side) * (n_row - 1 - t)
        inside = (t <= 2 * paired).astype(jnp.int32)
        return inside * near + (1 - inside) * far

    def block_to(row):
        return copy(mine, held.at[r], line_send.at[row], line_recv.at[r], row, col)

    def feats_to(column):
        return copy(
            mine.at[0:feats], plane.at[col], plane_send.at[column], plane_recv.at[col], r, column
        )

    def block_from(row):
        slot = held.at[row]
        return copy(slot, slot, line_send.at[row], line_recv.at[row], row, col)

    def feats_from(column):
        slot = plane.at[column]
        return copy(slot, slot, plane_send.at[column], plane_recv.at[column], r, column)

    def part_to(column):
        return copy(
            part_out.at[column], part_in.at[col], part_send.at[column], part_recv.at[col], r, column
        )

    def part_from(column):
        slot = part_in.at[column]
        return copy(slot, slot, part_send.at[column], part_recv.at[column], r, column)

    mate = q * 2 + (1 - col % 2)
    block_to(order(1)).start()
    feats_to(mate).start()

    @pl.loop(2, n_row)
    def _(t):
        block_to(order(t)).start()

    @pl.loop(1, n_col)
    def _(k):
        @pl.when(on_plane(k) != mate)
        def _():
            feats_to(on_plane(k)).start()

    plane[col] = mine[0:feats, :]
    inv_two = 0.5 / (ls_ref[0] * ls_ref[0])

    def chunk(k):
        if n_quad != 4:
            return (q + k) % n_quad
        x, y = q % 2, q // 2
        return (q, y * 2 + 1 - x, (1 - y) * 2 + x, 3 - q)[k]

    def each_chunk(use, backwards=False):
        if n_quad == 4:
            for k in (3, 2, 1, 0) if backwards else range(4):
                use(chunk(k), k == 0)
        else:
            use(q, True)

            @pl.loop(1, n_quad)
            def _(k):
                use(chunk(k), False)

    def prepare(quad):
        for half in range(2):
            x = jnp.transpose(plane[2 * quad + half])
            rows = slice(half * width, (half + 1) * width)
            own_sq[quad, rows, :] = jnp.broadcast_to(
                jnp.sum(x * x, axis=1, keepdims=True), (width, width)
            )
            high, middle, low = split_three(-2.0 * x)
            own_split[quad, rows, :] = jnp.concatenate([high, high, middle, high, low, middle], 1)

    def open_block(row):
        block = held.at[row]
        x = block[0:feats, :]
        high, middle, low = split_three(x)
        stack = jnp.concatenate([high, middle, high, low, high, middle], 0)
        sq = jnp.sum(x * x, axis=0, keepdims=True)
        rhs = jnp.concatenate(
            [block[feats:, :], jnp.zeros((lhs_rows - rhs_rows, width), F32)], 0
        )
        b_high, b_middle, b_low = split_three(rhs)
        return (
            stack,
            sq,
            jnp.concatenate([b_high, b_middle, b_low], 0),
            jnp.concatenate([b_high, b_middle], 0),
        )

    def absorb(opened, quad):
        stack, sq, lhs_three, lhs_two = opened
        dots = jnp.dot(own_split[quad], stack, preferred_element_type=F32)
        dist = jnp.maximum((own_sq[quad] + sq) + dots, 0.0)
        kern = jnp.exp(dist * (-inv_two))
        both = jnp.concatenate([kern, kern * dist], 0)
        both_high = both.astype(BF16)
        both_middle = (both - both_high.astype(F32)).astype(BF16)
        first = lax.dot_general(lhs_three, both_high, NT, preferred_element_type=F32)
        second = lax.dot_general(lhs_two, both_middle, NT, preferred_element_type=F32)
        small = (first[2 * lhs_rows :] + second[lhs_rows:]) + (
            first[lhs_rows : 2 * lhs_rows] + second[:lhs_rows]
        )
        acc[quad] += first[:lhs_rows] + small

    def send_parts(quad, is_own):
        for half in range(2):
            column = 2 * quad + half
            part_out[column, 0:rhs_rows, :] = acc[quad, 0:rhs_rows, half * width : (half + 1) * width]
            part_out[column, rhs_rows:, :] = acc[
                quad, 0:n_probes, (2 + half) * width : (3 + half) * width
            ]
        if is_own:
            part_to(mate).start()
        else:
            part_to(2 * quad).start()
            part_to(2 * quad + 1).start()

    opened = open_block(r)

    def first_use(quad, is_own):
        if is_own:
            feats_from(mate).wait_recv()
        else:
            feats_from(2 * quad).wait_recv()
            feats_from(2 * quad + 1).wait_recv()
        prepare(quad)
        absorb(opened, quad)
        if n_row == 1:
            send_parts(quad, is_own)

    each_chunk(first_use)
    for t in range(1, n_row):
        row = order(t)
        block_from(row).wait_recv()
        opened = open_block(row)

        def use(quad, is_own, opened=opened, last=t == n_row - 1):
            absorb(opened, quad)
            if last:
                send_parts(quad, is_own)

        each_chunk(use, backwards=True)

    part_in[col] = part_out[col]
    rhs = mine[feats:, :]
    scale = os_ref[0]
    noise = no_ref[0]

    @pl.loop(1, n_col)
    def _(k):
        part_from(on_plane(k)).wait_recv()

    whole = jnp.sum(part_in[...], axis=0)
    eb = whole[0:rhs_rows]
    ed = whole[rhs_rows:]
    kb = scale * eb + noise * rhs
    terms = [rhs * rhs, rhs * kb, kb * kb]
    lanes = up_to(3 * rhs_rows, 128)
    if lanes > 3 * rhs_rows:
        terms.append(jnp.zeros((lanes - 3 * rhs_rows, width), F32))
    row_sums = lax.dot_general(
        jnp.ones((8, width), F32),
        jnp.concatenate(terms, 0),
        NT,
        precision=lax.Precision.HIGHEST,
        preferred_element_type=F32,
    )
    line_sums[r] = row_sums[0:1]

    def line_share(k):
        row = on_line(k)
        return copy(line_sums.at[r], line_sums.at[r], ls_send.at[row], ls_recv.at[r], row, col)

    def plane_share(k):
        column = on_plane(k)
        return copy(
            plane_sums.at[col], plane_sums.at[col], ps_send.at[column], ps_recv.at[col], r, column
        )

    for k in range(1, n_row):
        line_share(k).start()

    tall = n_probes + 1
    short_out[0] = (scale / (ls_ref[0] * ls_ref[0] * ls_ref[0])) * ed
    short_out[1] = eb[0:n_probes]
    stores = [
        pltpu.make_async_copy(tall_out.at[0], sol_hbm, store_sem.at[0]),
        pltpu.make_async_copy(tall_out.at[1], res_hbm, store_sem.at[1]),
        pltpu.make_async_copy(tall_out.at[2], dir_hbm, store_sem.at[2]),
        pltpu.make_async_copy(short_out.at[0], len_hbm, store_sem.at[3]),
        pltpu.make_async_copy(short_out.at[1], scl_hbm, store_sem.at[4]),
    ]
    stores[3].start()
    stores[4].start()

    @pl.loop(1, n_row)
    def _(k):
        row = on_line(k)
        slot = line_sums.at[row]
        copy(slot, slot, ls_send.at[row], ls_recv.at[row], row, col).wait_recv()

    plane_sums[col] = jnp.sum(line_sums[...], axis=0)

    @pl.loop(1, n_col)
    def _(k):
        plane_share(k).start()

    @pl.loop(1, n_col)
    def _(k):
        column = on_plane(k)
        slot = plane_sums.at[column]
        copy(slot, slot, ps_send.at[column], ps_recv.at[column], r, column).wait_recv()

    total = jnp.sum(plane_sums[...], axis=0)
    lane = lax.broadcasted_iota(jnp.int32, (rhs_rows, lanes), 1)
    sub = lax.broadcasted_iota(jnp.int32, (rhs_rows, lanes), 0)

    def column_of(index):
        picked = jnp.where(lane == sub + index * rhs_rows, total, 0.0)
        return jnp.sum(picked, axis=1, keepdims=True)

    norm_old, curv, kb_sq = column_of(0), column_of(1), column_of(2)
    alpha = norm_old / curv
    norm_new = jnp.maximum(alpha * (alpha * kb_sq) - norm_old, 0.0)
    beta = norm_new / norm_old
    residual = rhs - alpha * kb
    for index, value in enumerate((alpha * rhs, residual, residual + beta * rhs)):
        tall_out[index, 0:1, :] = value[n_probes:tall]
        tall_out[index, 1:tall, :] = value[0:n_probes]
        stores[index].start()

    @pl.loop(1, n_row)
    def _(k):
        block_to(on_line(k)).wait_send()
        line_share(k).wait_send()

    @pl.loop(1, n_col)
    def _(k):
        feats_to(on_plane(k)).wait_send()
        part_to(on_plane(k)).wait_send()
        plane_share(k).wait_send()

    for store in stores:
        store.wait()


def hand_over(n_arrays, *refs):
    moves = [
        pltpu.make_async_copy(refs[i], refs[n_arrays + i], refs[2 * n_arrays].at[i])
        for i in range(n_arrays)
    ]
    for move in moves:
        move.start()
    for move in moves:
        move.wait()


def shards(n_row, n_col, points, targets, probes, lengthscale, outputscale, noise):
    feats, width = points.shape
    n_probes = probes.shape[0]
    n_quad = n_col // 2
    rhs_rows = up_to(n_probes + 1, 8)
    lhs_rows = up_to(n_probes + 1, 16)
    rows = feats + rhs_rows
    lanes = up_to(3 * rhs_rows, 128)
    smem = pl.BlockSpec(memory_space=pltpu.SMEM)
    hbm = pl.BlockSpec(memory_space=pltpu.HBM)
    dma = pltpu.SemaphoreType.DMA
    tall = jax.ShapeDtypeStruct((n_probes + 1, width), F32)
    short = jax.ShapeDtypeStruct((n_probes, width), F32)
    outs = (tall, tall, tall, short, short)
    results = pl.pallas_call(
        functools.partial(kernel, n_row, n_col, feats, n_probes),
        out_shape=outs,
        in_specs=[hbm, hbm, hbm, smem, smem, smem],
        out_specs=(hbm,) * len(outs),
        scratch_shapes=[
            pltpu.VMEM((n_row, rows, width), F32),
            pltpu.VMEM((n_col, feats, width), F32),
            pltpu.VMEM((1, width), F32),
            pltpu.VMEM((n_quad, 2 * width, 6 * feats), BF16),
            pltpu.VMEM((n_quad, 2 * width, width), F32),
            pltpu.VMEM((n_quad, lhs_rows, 4 * width), F32),
            pltpu.VMEM((n_col, rhs_rows + n_probes, width), F32),
            pltpu.VMEM((n_col, rhs_rows + n_probes, width), F32),
            pltpu.VMEM((n_row, 1, lanes), F32),
            pltpu.VMEM((n_col, 1, lanes), F32),
            dma((3,)),
            dma((n_row,)),
            dma((n_row,)),
            dma((n_col,)),
            dma((n_col,)),
            dma((n_col,)),
            dma((n_col,)),
            dma((n_row,)),
            dma((n_row,)),
            dma((n_col,)),
            dma((n_col,)),
            pltpu.VMEM((3, n_probes + 1, width), F32),
            pltpu.VMEM((2, n_probes, width), F32),
            dma((len(outs),)),
        ],
        compiler_params=pltpu.CompilerParams(
            collective_id=0, has_side_effects=True, vmem_limit_bytes=60 << 20
        ),
    )(points, targets[None, :], probes, lengthscale, outputscale, noise)
    return pl.pallas_call(
        functools.partial(hand_over, len(outs)),
        out_shape=outs,
        in_specs=[hbm] * len(outs),
        out_specs=(hbm,) * len(outs),
        scratch_shapes=[dma((len(outs),))],
        compiler_params=pltpu.CompilerParams(vmem_limit_bytes=60 << 20),
    )(*results)


def solution(mesh):
    split = ("row", "col")
    wide = P(None, split)
    return jax.shard_map(
        functools.partial(shards, mesh.shape["row"], mesh.shape["col"]),
        mesh=mesh,
        in_specs=(wide, P(split), wide, P(), P(), P()),
        out_specs=(wide,) * 5,
        check_vma=False,
    )
```

```python
import functools

import jax
import jax.numpy as jnp
from jax import lax
from jax.experimental import pallas as pl
from jax.experimental.pallas import tpu as pltpu
from jax.sharding import PartitionSpec as P

MESH = pl.DeviceIdType.MESH
F32 = jnp.float32
BF16 = jnp.bfloat16
NT = (((1,), (1,)), ((), ()))


def up_to(value, multiple):
    return (value + multiple - 1) // multiple * multiple


def split_three(value):
    high = value.astype(BF16)
    rest = value - high.astype(F32)
    middle = rest.astype(BF16)
    low = (rest - middle.astype(F32)).astype(BF16)
    return high, middle, low


def each(first, last, use):
    if last - first <= 7:
        for k in range(first, last):
            use(k)
    else:
        pl.loop(first, last)(use)


def kernel(
    n_row,
    n_col,
    feats,
    n_probes,
    x_hbm,
    t_hbm,
    p_hbm,
    ls_ref,
    os_ref,
    no_ref,
    out_ref,
    held,
    other,
    plane,
    targets,
    own_split,
    own_sq,
    acc,
    part_out,
    part_in,
    line_sums,
    plane_sums,
    load_sem,
    line_send,
    line_recv,
    mate_send,
    mate_recv,
    plane_send,
    plane_recv,
    part_send,
    part_recv,
    ls_send,
    ls_recv,
    ps_send,
    ps_recv,
):
    r = lax.axis_index("row")
    col = lax.axis_index("col")
    n_quad = n_col // 2
    q = col // 2
    width = x_hbm.shape[1]
    rhs_rows = up_to(n_probes + 1, 8)
    lhs_rows = up_to(n_probes + 1, 16)

    mine = held.at[r]
    loads = [
        pltpu.make_async_copy(x_hbm, mine.at[0:feats], load_sem.at[0]),
        pltpu.make_async_copy(p_hbm, mine.at[feats : feats + n_probes], load_sem.at[1]),
        pltpu.make_async_copy(t_hbm, targets, load_sem.at[2]),
    ]
    for load in loads:
        load.start()

    barrier = pltpu.get_barrier_semaphore()

    def on_line(k):
        return (r + k) % n_row

    def on_plane(k):
        return (col + k) % n_col

    def greet(row, column):
        pl.semaphore_signal(
            barrier, inc=1, device_id={"row": row, "col": column}, device_id_type=MESH
        )

    each(1, n_row, lambda k: greet(on_line(k), col))
    each(1, n_col, lambda k: greet(r, on_plane(k)))

    acc[...] = jnp.zeros_like(acc)
    for load in loads:
        load.wait()
    mine[feats + n_probes :, :] = jnp.concatenate(
        [targets[...], jnp.zeros((rhs_rows - n_probes - 1, width), F32)], 0
    )
    pl.semaphore_wait(barrier, n_row + n_col - 2)

    def copy(src, dst, send, recv, row, column):
        return pltpu.make_async_remote_copy(
            src_ref=src, dst_ref=dst, send_sem=send, recv_sem=recv,
            device_id={"row": row, "col": column}, device_id_type=MESH,
        )

    paired = jnp.minimum(r, n_row - 1 - r)
    low_side = (2 * r < n_row).astype(jnp.int32)

    def order(t):
        near = r + (t % 2) * (-((t + 1) // 2)) + (1 - t % 2) * (t // 2)
        far = low_side * t + (1 - low_side) * (n_row - 1 - t)
        inside = (t <= 2 * paired).astype(jnp.int32)
        return inside * near + (1 - inside) * far

    def block_to(row):
        return copy(mine, held.at[r], line_send.at[row], line_recv.at[r], row, col)

    def block_from(row):
        slot = held.at[row]
        return copy(slot, slot, line_send.at[row], line_recv.at[row], row, col)

    mate = q * 2 + (1 - col % 2)

    def to_mate(row):
        return copy(held.at[row], other.at[row], mate_send.at[row], mate_recv.at[row], r, mate)

    def feats_to(quad):
        return copy(
            mine.at[0:feats], plane.at[q], plane_send.at[quad], plane_recv.at[q],
            r, quad * 2 + col % 2,
        )

    def feats_from(quad):
        slot = plane.at[quad]
        return copy(slot, slot, plane_send.at[quad], plane_recv.at[quad], r, quad * 2 + col % 2)

    def part_to(quad):
        return copy(
            part_out.at[quad], part_in.at[q], part_send.at[quad], part_recv.at[q],
            r, quad * 2 + col % 2,
        )

    def part_from(quad):
        slot = part_in.at[quad]
        return copy(slot, slot, part_send.at[quad], part_recv.at[quad], r, quad * 2 + col % 2)

    def chunk(k):
        if n_quad != 4:
            return (q + k) % n_quad
        x, y = q % 2, q // 2
        return (q, y * 2 + 1 - x, (1 - y) * 2 + x, 3 - q)[k]

    to_mate(r).start()
    block_to(order(1)).start()
    each(1, n_quad, lambda k: feats_to(chunk(k)).start())
    each(2, n_row, lambda t: block_to(order(t)).start())
    plane[q] = mine[0:feats, :]
    inv_two = 0.5 / (ls_ref[0] * ls_ref[0])

    def prepare(k):
        x = jnp.transpose(plane[chunk(k)])
        rows = pl.ds(pl.multiple_of(k * width, width), width)
        own_sq[rows, :] = jnp.broadcast_to(
            jnp.sum(x * x, axis=1, keepdims=True), (width, 2 * width)
        )
        high, middle, low = split_three(-2.0 * x)
        own_split[rows, :] = jnp.concatenate([high, high, middle, high, low, middle], 1)

    def open_pair(row):
        x = jnp.concatenate([held[row, 0:feats, :], other[row, 0:feats, :]], 1)
        high, middle, low = split_three(x)
        stack = jnp.concatenate([high, middle, high, low, high, middle], 0)
        sq = jnp.sum(x * x, axis=0, keepdims=True)
        rhs = jnp.concatenate([held[row, feats:, :], other[row, feats:, :]], 1)
        rhs = jnp.concatenate([rhs, jnp.zeros((lhs_rows - rhs_rows, 2 * width), F32)], 0)
        b_high, b_middle, b_low = split_three(rhs)
        return (
            stack,
            sq,
            jnp.concatenate([b_high, b_middle, b_low], 0),
            jnp.concatenate([b_high, b_middle], 0),
        )

    group = 2 if n_quad % 2 == 0 else 1
    span = group * width

    def absorb(opened, index):
        stack, sq, lhs_three, lhs_two = opened
        rows = pl.ds(pl.multiple_of(index * span, span), span)
        dots = jnp.dot(own_split[rows, :], stack, preferred_element_type=F32)
        dist = jnp.maximum((own_sq[rows, :] + sq) + dots, 0.0)
        kern = jnp.exp(dist * (-inv_two))
        both = jnp.concatenate([kern, kern * dist], 0)
        both_high = both.astype(BF16)
        both_middle = (both - both_high.astype(F32)).astype(BF16)
        first = lax.dot_general(lhs_three, both_high, NT, preferred_element_type=F32)
        second = lax.dot_general(lhs_two, both_middle, NT, preferred_element_type=F32)
        small = (first[2 * lhs_rows :] + second[lhs_rows:]) + (
            first[lhs_rows : 2 * lhs_rows] + second[:lhs_rows]
        )
        acc[index] += first[:lhs_rows] + small

    def send_parts(index, own_too):
        for j in range(group):
            quad = chunk(index * group + j)
            part_out[quad, 0:rhs_rows, :] = acc[index, 0:rhs_rows, j * width : (j + 1) * width]
            part_out[quad, rhs_rows:, :] = acc[
                index, 0:n_probes, span + j * width : span + (j + 1) * width
            ]
            if not (own_too and j == 0):
                part_to(quad).start()

    prepare(0)

    def prepare_other(k):
        feats_from(chunk(k)).wait_recv()
        prepare(k)

    each(1, n_quad, prepare_other)
    n_groups = n_quad // group
    for t in range(n_row):
        if t + 1 < n_row:
            block_from(order(t + 1)).wait_recv()
            to_mate(order(t + 1)).start()
        row = order(t)
        arrival = other.at[row]
        copy(arrival, arrival, mate_send.at[row], mate_recv.at[row], r, mate).wait_recv()
        opened = open_pair(row)
        if t < n_row - 1:
            each(0, n_groups, lambda index: absorb(opened, index))
        else:

            def finish(index, own_too=False):
                absorb(opened, index)
                send_parts(index, own_too)

            each(1, n_groups, finish)
            finish(0, True)

    part_in[q] = part_out[q]
    rhs = mine[feats:, :]
    scale = os_ref[0]
    noise = no_ref[0]

    each(1, n_quad, lambda k: part_from(chunk(k)).wait_recv())

    whole = jnp.sum(part_in[...], axis=0)
    eb = whole[0:rhs_rows]
    ed = whole[rhs_rows:]
    kb = scale * eb + noise * rhs
    terms = [rhs * rhs, rhs * kb, kb * kb]
    lanes = up_to(3 * rhs_rows, 128)
    if lanes > 3 * rhs_rows:
        terms.append(jnp.zeros((lanes - 3 * rhs_rows, width), F32))
    row_sums = lax.dot_general(
        jnp.ones((8, width), F32),
        jnp.concatenate(terms, 0),
        NT,
        precision=lax.Precision.HIGHEST,
        preferred_element_type=F32,
    )
    line_sums[r] = row_sums[0:1]

    def line_share(k):
        row = on_line(k)
        return copy(line_sums.at[r], line_sums.at[r], ls_send.at[row], ls_recv.at[r], row, col)

    def plane_share(k):
        column = on_plane(k)
        return copy(
            plane_sums.at[col], plane_sums.at[col], ps_send.at[column], ps_recv.at[col], r, column
        )

    each(1, n_row, lambda k: line_share(k).start())

    tall = n_probes + 1
    out_ref[3, 0:n_probes, :] = (scale / (ls_ref[0] * ls_ref[0] * ls_ref[0])) * ed
    out_ref[4, 0:n_probes, :] = eb[0:n_probes]

    def line_arrived(k):
        row = on_line(k)
        slot = line_sums.at[row]
        copy(slot, slot, ls_send.at[row], ls_recv.at[row], row, col).wait_recv()

    each(1, n_row, line_arrived)

    plane_sums[col] = jnp.sum(line_sums[...], axis=0)

    each(1, n_col, lambda k: plane_share(k).start())

    def plane_arrived(k):
        column = on_plane(k)
        slot = plane_sums.at[column]
        copy(slot, slot, ps_send.at[column], ps_recv.at[column], r, column).wait_recv()

    each(1, n_col, plane_arrived)

    total = jnp.sum(plane_sums[...], axis=0)
    lane = lax.broadcasted_iota(jnp.int32, (rhs_rows, lanes), 1)
    sub = lax.broadcasted_iota(jnp.int32, (rhs_rows, lanes), 0)

    def column_of(index):
        picked = jnp.where(lane == sub + index * rhs_rows, total, 0.0)
        return jnp.sum(picked, axis=1, keepdims=True)

    norm_old, curv, kb_sq = column_of(0), column_of(1), column_of(2)
    alpha = norm_old / curv
    norm_new = jnp.maximum(alpha * (alpha * kb_sq) - norm_old, 0.0)
    beta = norm_new / norm_old
    residual = rhs - alpha * kb
    for index, value in enumerate((alpha * rhs, residual, residual + beta * rhs)):
        out_ref[index, 0:1, :] = value[n_probes:tall]
        out_ref[index, 1:tall, :] = value[0:n_probes]

    def line_left(k):
        block_to(on_line(k)).wait_send()
        line_share(k).wait_send()

    def quad_left(k):
        feats_to(chunk(k)).wait_send()
        part_to(chunk(k)).wait_send()

    each(1, n_row, line_left)
    each(0, n_row, lambda row: to_mate(row).wait_send())
    each(1, n_quad, quad_left)
    each(1, n_col, lambda k: plane_share(k).wait_send())


def unpack(packed, sol_ref, res_ref, dir_ref, len_ref, scl_ref):
    for index, ref in enumerate((sol_ref, res_ref, dir_ref, len_ref, scl_ref)):
        ref[...] = packed[index, 0 : ref.shape[0], :]


def shards(n_row, n_col, points, targets, probes, lengthscale, outputscale, noise):
    feats, width = points.shape
    n_probes = probes.shape[0]
    n_quad = n_col // 2
    rhs_rows = up_to(n_probes + 1, 8)
    lhs_rows = up_to(n_probes + 1, 16)
    rows = feats + rhs_rows
    group = 2 if n_quad % 2 == 0 else 1
    lanes = up_to(3 * rhs_rows, 128)
    vmem = pl.BlockSpec(memory_space=pltpu.VMEM)
    smem = pl.BlockSpec(memory_space=pltpu.SMEM)
    hbm = pl.BlockSpec(memory_space=pltpu.HBM)
    dma = pltpu.SemaphoreType.DMA
    packed = pl.pallas_call(
        functools.partial(kernel, n_row, n_col, feats, n_probes),
        out_shape=jax.ShapeDtypeStruct((5, rhs_rows, width), F32),
        in_specs=[hbm, hbm, hbm, smem, smem, smem],
        out_specs=vmem,
        scratch_shapes=[
            pltpu.VMEM((n_row, rows, width), F32),
            pltpu.VMEM((n_row, rows, width), F32),
            pltpu.VMEM((n_quad, feats, width), F32),
            pltpu.VMEM((1, width), F32),
            pltpu.VMEM((n_quad * width, 6 * feats), BF16),
            pltpu.VMEM((n_quad * width, 2 * width), F32),
            pltpu.VMEM((n_quad // group, lhs_rows, 2 * group * width), F32),
            pltpu.VMEM((n_quad, rhs_rows + n_probes, width), F32),
            pltpu.VMEM((n_quad, rhs_rows + n_probes, width), F32),
            pltpu.VMEM((n_row, 1, lanes), F32),
            pltpu.VMEM((n_col, 1, lanes), F32),
            dma((3,)),
            dma((n_row,)),
            dma((n_row,)),
            dma((n_row,)),
            dma((n_row,)),
            dma((n_quad,)),
            dma((n_quad,)),
            dma((n_quad,)),
            dma((n_quad,)),
            dma((n_row,)),
            dma((n_row,)),
            dma((n_col,)),
            dma((n_col,)),
        ],
        compiler_params=pltpu.CompilerParams(
            collective_id=0, has_side_effects=True, vmem_limit_bytes=60 << 20
        ),
    )(points, targets[None, :], probes, lengthscale, outputscale, noise)
    tall = jax.ShapeDtypeStruct((n_probes + 1, width), F32)
    short = jax.ShapeDtypeStruct((n_probes, width), F32)
    return pl.pallas_call(
        unpack,
        out_shape=(tall, tall, tall, short, short),
        in_specs=[vmem],
        out_specs=(vmem,) * 5,
    )(packed)


def solution(mesh):
    split = ("row", "col")
    wide = P(None, split)
    return jax.shard_map(
        functools.partial(shards, mesh.shape["row"], mesh.shape["col"]),
        mesh=mesh,
        in_specs=(wide, P(split), wide, P(), P(), P()),
        out_specs=(wide,) * 5,
        check_vma=False,
    )
```

```python
import functools

import jax
import jax.numpy as jnp
from jax import lax
from jax.experimental import pallas as pl
from jax.experimental.pallas import tpu as pltpu
from jax.sharding import PartitionSpec as P

MESH = pl.DeviceIdType.MESH
F32 = jnp.float32
BF16 = jnp.bfloat16
NT = (((1,), (1,)), ((), ()))


def up_to(value, multiple):
    return (value + multiple - 1) // multiple * multiple


def split_three(value):
    high = value.astype(BF16)
    rest = value - high.astype(F32)
    middle = rest.astype(BF16)
    low = (rest - middle.astype(F32)).astype(BF16)
    return high, middle, low


def each(first, last, use):
    if last - first <= 7:
        for k in range(first, last):
            use(k)
    else:
        pl.loop(first, last)(use)


def kernel(
    n_row,
    n_col,
    feats,
    n_probes,
    x_hbm,
    t_hbm,
    p_hbm,
    ls_ref,
    os_ref,
    no_ref,
    out_ref,
    held,
    other,
    plane,
    targets,
    own_split,
    own_sq,
    acc,
    part_out,
    part_in,
    line_sums,
    plane_sums,
    load_sem,
    up_send,
    line_send,
    line_recv,
    mate_send,
    mate_recv,
    plane_send,
    plane_recv,
    part_send,
    part_recv,
    ls_send,
    ls_recv,
    ps_send,
    ps_recv,
):
    r = lax.axis_index("row")
    col = lax.axis_index("col")
    n_quad = n_col // 2
    q = col // 2
    width = x_hbm.shape[1]
    rhs_rows = up_to(n_probes + 1, 8)
    lhs_rows = up_to(n_probes + 1, 16)

    mine = held.at[r]
    loads = [
        pltpu.make_async_copy(x_hbm, mine.at[0:feats], load_sem.at[0]),
        pltpu.make_async_copy(p_hbm, mine.at[feats : feats + n_probes], load_sem.at[1]),
        pltpu.make_async_copy(t_hbm, targets, load_sem.at[2]),
    ]
    for load in loads:
        load.start()

    barrier = pltpu.get_barrier_semaphore()

    def on_line(k):
        return (r + k) % n_row

    def on_plane(k):
        return (col + k) % n_col

    def greet(row, column):
        pl.semaphore_signal(
            barrier, inc=1, device_id={"row": row, "col": column}, device_id_type=MESH
        )

    def greet_line(k):
        row = on_line(k)

        @pl.when(jnp.logical_or(row > r, row == r - 1))
        def _():
            greet(row, col)

    each(1, n_row, greet_line)
    each(1, n_col, lambda k: greet(r, on_plane(k)))

    acc[...] = jnp.zeros_like(acc)
    for load in loads:
        load.wait()
    mine[feats + n_probes :, :] = jnp.concatenate(
        [targets[...], jnp.zeros((rhs_rows - n_probes - 1, width), F32)], 0
    )
    has_upper = (r + 1 < n_row).astype(jnp.int32)
    pl.semaphore_wait(barrier, r + has_upper + n_col - 1)

    def copy(src, dst, send, recv, row, column):
        return pltpu.make_async_remote_copy(
            src_ref=src, dst_ref=dst, send_sem=send, recv_sem=recv,
            device_id={"row": row, "col": column}, device_id_type=MESH,
        )

    def order(t):
        below = (t <= r).astype(jnp.int32)
        return below * (r - t) + (1 - below) * t

    def upward(row):
        slot = held.at[row]
        return copy(
            slot, slot, up_send.at[row], line_recv.at[row], jnp.minimum(r + 1, n_row - 1), col
        )

    def each_upward(row, use):
        @pl.when(jnp.logical_and(row <= r, r + 1 < n_row))
        def _():
            use(upward(row))

    def each_downward(k, use):
        @pl.when(k <= r)
        def _():
            use(block_to(jnp.maximum(r - k, 0)))

    def block_to(row):
        return copy(mine, held.at[r], line_send.at[row], line_recv.at[r], row, col)

    def block_from(row):
        slot = held.at[row]
        return copy(slot, slot, line_send.at[row], line_recv.at[row], row, col)

    mate = q * 2 + (1 - col % 2)

    def to_mate(row):
        return copy(held.at[row], other.at[row], mate_send.at[row], mate_recv.at[row], r, mate)

    def feats_to(quad):
        return copy(
            mine.at[0:feats], plane.at[q], plane_send.at[quad], plane_recv.at[q],
            r, quad * 2 + col % 2,
        )

    def feats_from(quad):
        slot = plane.at[quad]
        return copy(slot, slot, plane_send.at[quad], plane_recv.at[quad], r, quad * 2 + col % 2)

    def part_to(quad):
        return copy(
            part_out.at[quad], part_in.at[q], part_send.at[quad], part_recv.at[q],
            r, quad * 2 + col % 2,
        )

    def part_from(quad):
        slot = part_in.at[quad]
        return copy(slot, slot, part_send.at[quad], part_recv.at[quad], r, quad * 2 + col % 2)

    def chunk(k):
        if n_quad != 4:
            return (q + k) % n_quad
        x, y = q % 2, q // 2
        return (q, y * 2 + 1 - x, (1 - y) * 2 + x, 3 - q)[k]

    to_mate(r).start()
    each_upward(r, lambda moved: moved.start())
    each(1, n_quad, lambda k: feats_to(chunk(k)).start())
    each(1, n_row, lambda k: each_downward(k, lambda moved: moved.start()))
    plane[q] = mine[0:feats, :]
    inv_two = 0.5 / (ls_ref[0] * ls_ref[0])

    def prepare(k):
        x = jnp.transpose(plane[chunk(k)])
        rows = pl.ds(pl.multiple_of(k * width, width), width)
        own_sq[rows, :] = jnp.broadcast_to(
            jnp.sum(x * x, axis=1, keepdims=True), (width, 2 * width)
        )
        high, middle, low = split_three(-2.0 * x)
        own_split[rows, :] = jnp.concatenate([high, high, middle, high, low, middle], 1)

    def open_pair(row):
        x = jnp.concatenate([held[row, 0:feats, :], other[row, 0:feats, :]], 1)
        high, middle, low = split_three(x)
        stack = jnp.concatenate([high, middle, high, low, high, middle], 0)
        sq = jnp.sum(x * x, axis=0, keepdims=True)
        rhs = jnp.concatenate([held[row, feats:, :], other[row, feats:, :]], 1)
        rhs = jnp.concatenate([rhs, jnp.zeros((lhs_rows - rhs_rows, 2 * width), F32)], 0)
        b_high, b_middle, b_low = split_three(rhs)
        return (
            stack,
            sq,
            jnp.concatenate([b_high, b_middle, b_low], 0),
            jnp.concatenate([b_high, b_middle], 0),
        )

    group = 2 if n_quad % 2 == 0 else 1
    span = group * width

    def absorb(opened, index):
        stack, sq, lhs_three, lhs_two = opened
        rows = pl.ds(pl.multiple_of(index * span, span), span)
        dots = jnp.dot(own_split[rows, :], stack, preferred_element_type=F32)
        dist = jnp.maximum((own_sq[rows, :] + sq) + dots, 0.0)
        kern = jnp.exp(dist * (-inv_two))
        both = jnp.concatenate([kern, kern * dist], 0)
        both_high = both.astype(BF16)
        both_middle = (both - both_high.astype(F32)).astype(BF16)
        first = lax.dot_general(lhs_three, both_high, NT, preferred_element_type=F32)
        second = lax.dot_general(lhs_two, both_middle, NT, preferred_element_type=F32)
        small = (first[2 * lhs_rows :] + second[lhs_rows:]) + (
            first[lhs_rows : 2 * lhs_rows] + second[:lhs_rows]
        )
        acc[index] += first[:lhs_rows] + small

    def send_parts(index, own_too):
        for j in range(group):
            quad = chunk(index * group + j)
            part_out[quad, 0:rhs_rows, :] = acc[index, 0:rhs_rows, j * width : (j + 1) * width]
            part_out[quad, rhs_rows:, :] = acc[
                index, 0:n_probes, span + j * width : span + (j + 1) * width
            ]
            if not (own_too and j == 0):
                part_to(quad).start()

    prepare(0)

    def prepare_other(k):
        feats_from(chunk(k)).wait_recv()
        prepare(k)

    each(1, n_quad, prepare_other)
    n_groups = n_quad // group
    for t in range(n_row):
        if t + 1 < n_row:
            coming = order(t + 1)
            block_from(coming).wait_recv()
            each_upward(coming, lambda moved: moved.start())
            to_mate(coming).start()
        row = order(t)
        arrival = other.at[row]
        copy(arrival, arrival, mate_send.at[row], mate_recv.at[row], r, mate).wait_recv()
        opened = open_pair(row)
        if t < n_row - 1:
            each(0, n_groups, lambda index: absorb(opened, index))
        else:

            def finish(index, own_too=False):
                absorb(opened, index)
                send_parts(index, own_too)

            each(1, n_groups, finish)
            finish(0, True)

    part_in[q] = part_out[q]
    rhs = mine[feats:, :]
    scale = os_ref[0]
    noise = no_ref[0]

    each(1, n_quad, lambda k: part_from(chunk(k)).wait_recv())

    whole = jnp.sum(part_in[...], axis=0)
    eb = whole[0:rhs_rows]
    ed = whole[rhs_rows:]
    kb = scale * eb + noise * rhs
    terms = [rhs * rhs, rhs * kb, kb * kb]
    lanes = up_to(3 * rhs_rows, 128)
    if lanes > 3 * rhs_rows:
        terms.append(jnp.zeros((lanes - 3 * rhs_rows, width), F32))
    row_sums = lax.dot_general(
        jnp.ones((8, width), F32),
        jnp.concatenate(terms, 0),
        NT,
        precision=lax.Precision.HIGHEST,
        preferred_element_type=F32,
    )
    line_sums[r] = row_sums[0:1]

    def line_share(k):
        row = on_line(k)
        return copy(line_sums.at[r], line_sums.at[r], ls_send.at[row], ls_recv.at[r], row, col)

    def plane_share(k):
        column = on_plane(k)
        return copy(
            plane_sums.at[col], plane_sums.at[col], ps_send.at[column], ps_recv.at[col], r, column
        )

    each(1, n_row, lambda k: line_share(k).start())

    tall = n_probes + 1
    out_ref[3, 0:n_probes, :] = (scale / (ls_ref[0] * ls_ref[0] * ls_ref[0])) * ed
    out_ref[4, 0:n_probes, :] = eb[0:n_probes]

    def line_arrived(k):
        row = on_line(k)
        slot = line_sums.at[row]
        copy(slot, slot, ls_send.at[row], ls_recv.at[row], row, col).wait_recv()

    each(1, n_row, line_arrived)

    plane_sums[col] = jnp.sum(line_sums[...], axis=0)

    each(1, n_col, lambda k: plane_share(k).start())

    def plane_arrived(k):
        column = on_plane(k)
        slot = plane_sums.at[column]
        copy(slot, slot, ps_send.at[column], ps_recv.at[column], r, column).wait_recv()

    each(1, n_col, plane_arrived)

    total = jnp.sum(plane_sums[...], axis=0)
    lane = lax.broadcasted_iota(jnp.int32, (rhs_rows, lanes), 1)
    sub = lax.broadcasted_iota(jnp.int32, (rhs_rows, lanes), 0)

    def column_of(index):
        picked = jnp.where(lane == sub + index * rhs_rows, total, 0.0)
        return jnp.sum(picked, axis=1, keepdims=True)

    norm_old, curv, kb_sq = column_of(0), column_of(1), column_of(2)
    alpha = norm_old / curv
    norm_new = jnp.maximum(alpha * (alpha * kb_sq) - norm_old, 0.0)
    beta = norm_new / norm_old
    residual = rhs - alpha * kb
    for index, value in enumerate((alpha * rhs, residual, residual + beta * rhs)):
        out_ref[index, 0:1, :] = value[n_probes:tall]
        out_ref[index, 1:tall, :] = value[0:n_probes]

    def line_left(k):
        each_downward(k, lambda moved: moved.wait_send())
        line_share(k).wait_send()

    def quad_left(k):
        feats_to(chunk(k)).wait_send()
        part_to(chunk(k)).wait_send()

    each(1, n_row, line_left)
    each(0, n_row, lambda row: to_mate(row).wait_send())
    each(0, n_row, lambda row: each_upward(row, lambda moved: moved.wait_send()))
    each(1, n_quad, quad_left)
    each(1, n_col, lambda k: plane_share(k).wait_send())


def unpack(packed, sol_ref, res_ref, dir_ref, len_ref, scl_ref):
    for index, ref in enumerate((sol_ref, res_ref, dir_ref, len_ref, scl_ref)):
        ref[...] = packed[index, 0 : ref.shape[0], :]


def shards(n_row, n_col, points, targets, probes, lengthscale, outputscale, noise):
    feats, width = points.shape
    n_probes = probes.shape[0]
    n_quad = n_col // 2
    rhs_rows = up_to(n_probes + 1, 8)
    lhs_rows = up_to(n_probes + 1, 16)
    rows = feats + rhs_rows
    group = 2 if n_quad % 2 == 0 else 1
    lanes = up_to(3 * rhs_rows, 128)
    vmem = pl.BlockSpec(memory_space=pltpu.VMEM)
    smem = pl.BlockSpec(memory_space=pltpu.SMEM)
    hbm = pl.BlockSpec(memory_space=pltpu.HBM)
    dma = pltpu.SemaphoreType.DMA
    packed = pl.pallas_call(
        functools.partial(kernel, n_row, n_col, feats, n_probes),
        out_shape=jax.ShapeDtypeStruct((5, rhs_rows, width), F32),
        in_specs=[hbm, hbm, hbm, smem, smem, smem],
        out_specs=vmem,
        scratch_shapes=[
            pltpu.VMEM((n_row, rows, width), F32),
            pltpu.VMEM((n_row, rows, width), F32),
            pltpu.VMEM((n_quad, feats, width), F32),
            pltpu.VMEM((1, width), F32),
            pltpu.VMEM((n_quad * width, 6 * feats), BF16),
            pltpu.VMEM((n_quad * width, 2 * width), F32),
            pltpu.VMEM((n_quad // group, lhs_rows, 2 * group * width), F32),
            pltpu.VMEM((n_quad, rhs_rows + n_probes, width), F32),
            pltpu.VMEM((n_quad, rhs_rows + n_probes, width), F32),
            pltpu.VMEM((n_row, 1, lanes), F32),
            pltpu.VMEM((n_col, 1, lanes), F32),
            dma((3,)),
            dma((n_row,)),
            dma((n_row,)),
            dma((n_row,)),
            dma((n_row,)),
            dma((n_row,)),
            dma((n_quad,)),
            dma((n_quad,)),
            dma((n_quad,)),
            dma((n_quad,)),
            dma((n_row,)),
            dma((n_row,)),
            dma((n_col,)),
            dma((n_col,)),
        ],
        compiler_params=pltpu.CompilerParams(
            collective_id=0, has_side_effects=True, vmem_limit_bytes=60 << 20
        ),
    )(points, targets[None, :], probes, lengthscale, outputscale, noise)
    tall = jax.ShapeDtypeStruct((n_probes + 1, width), F32)
    short = jax.ShapeDtypeStruct((n_probes, width), F32)
    return pl.pallas_call(
        unpack,
        out_shape=(tall, tall, tall, short, short),
        in_specs=[vmem],
        out_specs=(vmem,) * 5,
    )(packed)


def solution(mesh):
    split = ("row", "col")
    wide = P(None, split)
    return jax.shard_map(
        functools.partial(shards, mesh.shape["row"], mesh.shape["col"]),
        mesh=mesh,
        in_specs=(wide, P(split), wide, P(), P(), P()),
        out_specs=(wide,) * 5,
        check_vma=False,
    )
```

```python
import functools

import jax
import jax.numpy as jnp
from jax import lax
from jax.experimental import pallas as pl
from jax.experimental.pallas import tpu as pltpu
from jax.sharding import PartitionSpec as P

MESH = pl.DeviceIdType.MESH
F32 = jnp.float32
BF16 = jnp.bfloat16
NT = (((1,), (1,)), ((), ()))


def up_to(value, multiple):
    return (value + multiple - 1) // multiple * multiple


def split_three(value):
    high = value.astype(BF16)
    rest = value - high.astype(F32)
    middle = rest.astype(BF16)
    low = (rest - middle.astype(F32)).astype(BF16)
    return high, middle, low


def each(first, last, use):
    if last - first <= 7:
        for k in range(first, last):
            use(k)
    else:
        pl.loop(first, last)(use)


def kernel(
    n_row,
    n_col,
    feats,
    n_probes,
    x_hbm,
    t_hbm,
    p_hbm,
    ls_ref,
    os_ref,
    no_ref,
    out_ref,
    held,
    other,
    plane,
    targets,
    own_split,
    own_sq,
    acc,
    part_out,
    part_in,
    sums,
    load_sem,
    line_send,
    line_recv,
    mate_send,
    mate_recv,
    plane_send,
    plane_recv,
    part_send,
    part_recv,
    sum_send,
    sum_recv,
):
    r = lax.axis_index("row")
    col = lax.axis_index("col")
    n_quad = n_col // 2
    q = col // 2
    width = x_hbm.shape[1]
    rhs_rows = up_to(n_probes + 1, 8)
    lhs_rows = up_to(n_probes + 1, 16)

    mine = held.at[r]
    loads = [
        pltpu.make_async_copy(x_hbm, mine.at[0:feats], load_sem.at[0]),
        pltpu.make_async_copy(p_hbm, mine.at[feats : feats + n_probes], load_sem.at[1]),
        pltpu.make_async_copy(t_hbm, targets, load_sem.at[2]),
    ]
    for load in loads:
        load.start()

    barrier = pltpu.get_barrier_semaphore()

    def on_line(k):
        return lax.rem(r + k, n_row)

    def on_plane(k):
        return lax.rem(col + k, n_col)

    def greet(row, column):
        pl.semaphore_signal(
            barrier, inc=1, device_id={"row": row, "col": column}, device_id_type=MESH
        )

    each(1, n_row, lambda k: greet(on_line(k), col))
    each(1, n_col, lambda k: greet(r, on_plane(k)))

    acc[...] = jnp.zeros_like(acc)
    for load in loads:
        load.wait()
    mine[feats + n_probes :, :] = jnp.concatenate(
        [targets[...], jnp.zeros((rhs_rows - n_probes - 1, width), F32)], 0
    )
    pl.semaphore_wait(barrier, n_row + n_col - 2)

    def copy(src, dst, send, recv, row, column):
        return pltpu.make_async_remote_copy(
            src_ref=src, dst_ref=dst, send_sem=send, recv_sem=recv,
            device_id={"row": row, "col": column}, device_id_type=MESH,
        )

    paired = jnp.minimum(r, n_row - 1 - r)
    low_side = (2 * r < n_row).astype(jnp.int32)

    def order(t):
        near = r + (t % 2) * (-((t + 1) // 2)) + (1 - t % 2) * (t // 2)
        far = low_side * t + (1 - low_side) * (n_row - 1 - t)
        inside = (t <= 2 * paired).astype(jnp.int32)
        return inside * near + (1 - inside) * far

    def block_to(row):
        return copy(mine, held.at[r], line_send.at[row], line_recv.at[r], row, col)

    def block_from(row):
        slot = held.at[row]
        return copy(slot, slot, line_send.at[row], line_recv.at[row], row, col)

    mate = q * 2 + (1 - col % 2)

    def to_mate(row):
        return copy(held.at[row], other.at[row], mate_send.at[row], mate_recv.at[row], r, mate)

    def feats_to(quad):
        return copy(
            mine.at[0:feats], plane.at[q], plane_send.at[quad], plane_recv.at[q],
            r, quad * 2 + col % 2,
        )

    def feats_from(quad):
        slot = plane.at[quad]
        return copy(slot, slot, plane_send.at[quad], plane_recv.at[quad], r, quad * 2 + col % 2)

    def part_to(quad):
        return copy(
            part_out.at[quad], part_in.at[q], part_send.at[quad], part_recv.at[q],
            r, quad * 2 + col % 2,
        )

    def part_from(quad):
        slot = part_in.at[quad]
        return copy(slot, slot, part_send.at[quad], part_recv.at[quad], r, quad * 2 + col % 2)

    def chunk(k):
        if n_quad != 4:
            return (q + k) % n_quad
        x, y = q % 2, q // 2
        return (q, y * 2 + 1 - x, (1 - y) * 2 + x, 3 - q)[k]

    to_mate(r).start()
    block_to(order(1)).start()
    each(1, n_quad, lambda k: feats_to(chunk(k)).start())
    each(2, n_row, lambda t: block_to(order(t)).start())
    plane[q] = mine[0:feats, :]
    inv_two = 0.5 / (ls_ref[0] * ls_ref[0])

    def prepare(k):
        x = jnp.transpose(plane[chunk(k)])
        rows = pl.ds(pl.multiple_of(k * width, width), width)
        own_sq[rows, :] = jnp.broadcast_to(
            jnp.sum(x * x, axis=1, keepdims=True), (width, 2 * width)
        )
        high, middle, low = split_three(-2.0 * x)
        own_split[rows, :] = jnp.concatenate([high, high, middle, high, low, middle], 1)

    def open_pair(row):
        x = jnp.concatenate([held[row, 0:feats, :], other[row, 0:feats, :]], 1)
        high, middle, low = split_three(x)
        stack = jnp.concatenate([high, middle, high, low, high, middle], 0)
        sq = jnp.sum(x * x, axis=0, keepdims=True)
        rhs = jnp.concatenate([held[row, feats:, :], other[row, feats:, :]], 1)
        rhs = jnp.concatenate([rhs, jnp.zeros((lhs_rows - rhs_rows, 2 * width), F32)], 0)
        b_high, b_middle, b_low = split_three(rhs)
        return (
            stack,
            sq,
            jnp.concatenate([b_high, b_middle, b_low], 0),
            jnp.concatenate([b_high, b_middle], 0),
        )

    group = 2 if n_quad % 2 == 0 else 1
    span = group * width

    def absorb(opened, index):
        stack, sq, lhs_three, lhs_two = opened
        rows = pl.ds(pl.multiple_of(index * span, span), span)
        dots = jnp.dot(own_split[rows, :], stack, preferred_element_type=F32)
        dist = jnp.maximum((own_sq[rows, :] + sq) + dots, 0.0)
        kern = jnp.exp(dist * (-inv_two))
        both = jnp.concatenate([kern, kern * dist], 0)
        both_high = both.astype(BF16)
        both_middle = (both - both_high.astype(F32)).astype(BF16)
        first = lax.dot_general(lhs_three, both_high, NT, preferred_element_type=F32)
        second = lax.dot_general(lhs_two, both_middle, NT, preferred_element_type=F32)
        small = (first[2 * lhs_rows :] + second[lhs_rows:]) + (
            first[lhs_rows : 2 * lhs_rows] + second[:lhs_rows]
        )
        acc[index] += first[:lhs_rows] + small

    def send_parts(index, own_too):
        for j in range(group):
            quad = chunk(index * group + j)
            part_out[quad, 0:rhs_rows, :] = acc[index, 0:rhs_rows, j * width : (j + 1) * width]
            part_out[quad, rhs_rows:, :] = acc[
                index, 0:n_probes, span + j * width : span + (j + 1) * width
            ]
            if not (own_too and j == 0):
                part_to(quad).start()

    prepare(0)

    def prepare_other(k):
        feats_from(chunk(k)).wait_recv()
        prepare(k)

    each(1, n_quad, prepare_other)
    n_groups = n_quad // group
    for t in range(n_row):
        if t + 1 < n_row:
            block_from(order(t + 1)).wait_recv()
            to_mate(order(t + 1)).start()
        row = order(t)
        arrival = other.at[row]
        copy(arrival, arrival, mate_send.at[row], mate_recv.at[row], r, mate).wait_recv()
        opened = open_pair(row)
        if t < n_row - 1:
            each(0, n_groups, lambda index: absorb(opened, index))
        else:

            def finish(index, own_too=False):
                absorb(opened, index)
                send_parts(index, own_too)

            each(1, n_groups, finish)
            finish(0, True)

    part_in[q] = part_out[q]
    rhs = mine[feats:, :]
    scale = os_ref[0]
    noise = no_ref[0]

    each(1, n_quad, lambda k: part_from(chunk(k)).wait_recv())

    whole = jnp.sum(part_in[...], axis=0)
    eb = whole[0:rhs_rows]
    ed = whole[rhs_rows:]
    kb = scale * eb + noise * rhs
    terms = [rhs * rhs, rhs * kb, kb * kb]
    lanes = up_to(3 * rhs_rows, 128)
    if lanes > 3 * rhs_rows:
        terms.append(jnp.zeros((lanes - 3 * rhs_rows, width), F32))
    row_sums = lax.dot_general(
        jnp.ones((8, width), F32),
        jnp.concatenate(terms, 0),
        NT,
        precision=lax.Precision.HIGHEST,
        preferred_element_type=F32,
    )
    me = r * n_col + col
    n_devices = n_row * n_col
    sums[me] = row_sums[0:1]

    def share(k):
        peer = lax.rem(me + k, n_devices)
        return copy(
            sums.at[me], sums.at[me], sum_send.at[0], sum_recv.at[0],
            lax.div(peer, n_col), lax.rem(peer, n_col),
        )

    @pl.loop(1, n_devices)
    def _(k):
        share(k).start()

    tall = n_probes + 1
    out_ref[3, 0:n_probes, :] = (scale / (ls_ref[0] * ls_ref[0] * ls_ref[0])) * ed
    out_ref[4, 0:n_probes, :] = eb[0:n_probes]

    shares = sums.at[pl.ds(0, n_devices - 1)]
    all_shares = copy(shares, shares, sum_send.at[0], sum_recv.at[0], r, mate)
    all_shares.wait_recv()
    total = jnp.sum(sums[...], axis=0)
    lane = lax.broadcasted_iota(jnp.int32, (rhs_rows, lanes), 1)
    sub = lax.broadcasted_iota(jnp.int32, (rhs_rows, lanes), 0)

    def column_of(index):
        picked = jnp.where(lane == sub + index * rhs_rows, total, 0.0)
        return jnp.sum(picked, axis=1, keepdims=True)

    norm_old, curv, kb_sq = column_of(0), column_of(1), column_of(2)
    alpha = norm_old / curv
    norm_new = jnp.maximum(alpha * (alpha * kb_sq) - norm_old, 0.0)
    beta = norm_new / norm_old
    residual = rhs - alpha * kb
    for index, value in enumerate((alpha * rhs, residual, residual + beta * rhs)):
        out_ref[index, 0:1, :] = value[n_probes:tall]
        out_ref[index, 1:tall, :] = value[0:n_probes]

    def line_left(k):
        block_to(on_line(k)).wait_send()

    def quad_left(k):
        feats_to(chunk(k)).wait_send()
        part_to(chunk(k)).wait_send()

    each(1, n_row, line_left)
    each(0, n_row, lambda row: to_mate(row).wait_send())
    each(1, n_quad, quad_left)
    all_shares.wait_send()


def unpack(packed, sol_ref, res_ref, dir_ref, len_ref, scl_ref):
    for index, ref in enumerate((sol_ref, res_ref, dir_ref, len_ref, scl_ref)):
        ref[...] = packed[index, 0 : ref.shape[0], :]


def shards(n_row, n_col, points, targets, probes, lengthscale, outputscale, noise):
    feats, width = points.shape
    n_probes = probes.shape[0]
    n_quad = n_col // 2
    rhs_rows = up_to(n_probes + 1, 8)
    lhs_rows = up_to(n_probes + 1, 16)
    rows = feats + rhs_rows
    group = 2 if n_quad % 2 == 0 else 1
    lanes = up_to(3 * rhs_rows, 128)
    vmem = pl.BlockSpec(memory_space=pltpu.VMEM)
    smem = pl.BlockSpec(memory_space=pltpu.SMEM)
    hbm = pl.BlockSpec(memory_space=pltpu.HBM)
    dma = pltpu.SemaphoreType.DMA
    packed = pl.pallas_call(
        functools.partial(kernel, n_row, n_col, feats, n_probes),
        out_shape=jax.ShapeDtypeStruct((5, rhs_rows, width), F32),
        in_specs=[hbm, hbm, hbm, smem, smem, smem],
        out_specs=vmem,
        scratch_shapes=[
            pltpu.VMEM((n_row, rows, width), F32),
            pltpu.VMEM((n_row, rows, width), F32),
            pltpu.VMEM((n_quad, feats, width), F32),
            pltpu.VMEM((1, width), F32),
            pltpu.VMEM((n_quad * width, 6 * feats), BF16),
            pltpu.VMEM((n_quad * width, 2 * width), F32),
            pltpu.VMEM((n_quad // group, lhs_rows, 2 * group * width), F32),
            pltpu.VMEM((n_quad, rhs_rows + n_probes, width), F32),
            pltpu.VMEM((n_quad, rhs_rows + n_probes, width), F32),
            pltpu.VMEM((n_row * n_col, 1, lanes), F32),
            dma((3,)),
            dma((n_row,)),
            dma((n_row,)),
            dma((n_row,)),
            dma((n_row,)),
            dma((n_quad,)),
            dma((n_quad,)),
            dma((n_quad,)),
            dma((n_quad,)),
            dma((1,)),
            dma((1,)),
        ],
        compiler_params=pltpu.CompilerParams(
            collective_id=0, has_side_effects=True, vmem_limit_bytes=60 << 20
        ),
    )(points, targets[None, :], probes, lengthscale, outputscale, noise)
    tall = jax.ShapeDtypeStruct((n_probes + 1, width), F32)
    short = jax.ShapeDtypeStruct((n_probes, width), F32)
    return pl.pallas_call(
        unpack,
        out_shape=(tall, tall, tall, short, short),
        in_specs=[vmem],
        out_specs=(vmem,) * 5,
    )(packed)


def solution(mesh):
    split = ("row", "col")
    wide = P(None, split)
    return jax.shard_map(
        functools.partial(shards, mesh.shape["row"], mesh.shape["col"]),
        mesh=mesh,
        in_specs=(wide, P(split), wide, P(), P(), P()),
        out_specs=(wide,) * 5,
        check_vma=False,
    )
```

```python
import functools

import jax
import jax.numpy as jnp
from jax import lax
from jax.experimental import pallas as pl
from jax.experimental.pallas import tpu as pltpu
from jax.sharding import PartitionSpec as P

MESH = pl.DeviceIdType.MESH
F32 = jnp.float32
BF16 = jnp.bfloat16
NT = (((1,), (1,)), ((), ()))


def up_to(value, multiple):
    return (value + multiple - 1) // multiple * multiple


def split_three(value):
    high = value.astype(BF16)
    rest = value - high.astype(F32)
    middle = rest.astype(BF16)
    low = (rest - middle.astype(F32)).astype(BF16)
    return high, middle, low


def each(first, last, use):
    if last - first <= 8:
        for k in range(first, last):
            use(k)
    else:
        pl.loop(first, last)(use)


def kernel(
    n_row,
    n_col,
    feats,
    n_probes,
    x_hbm,
    t_hbm,
    p_hbm,
    ls_ref,
    os_ref,
    no_ref,
    out_ref,
    held,
    other,
    plane,
    targets,
    own_split,
    own_sq,
    acc,
    part_out,
    part_in,
    sums,
    load_sem,
    line_send,
    line_recv,
    mate_send,
    mate_recv,
    plane_send,
    plane_recv,
    part_send,
    part_recv,
    sum_send,
    sum_recv,
):
    r = lax.axis_index("row")
    col = lax.axis_index("col")
    n_quad = n_col // 2
    q = col // 2
    width = x_hbm.shape[1]
    rhs_rows = up_to(n_probes + 1, 8)
    lhs_rows = up_to(n_probes + 1, 16)

    mine = held.at[r]
    loads = [
        pltpu.make_async_copy(x_hbm, mine.at[0:feats], load_sem.at[0]),
        pltpu.make_async_copy(p_hbm, mine.at[feats : feats + n_probes], load_sem.at[1]),
        pltpu.make_async_copy(t_hbm, targets, load_sem.at[2]),
    ]
    for load in loads:
        load.start()

    barrier = pltpu.get_barrier_semaphore()

    def on_line(k):
        return lax.rem(r + k, n_row)

    def on_plane(k):
        return lax.rem(col + k, n_col)

    def greet(row, column):
        pl.semaphore_signal(
            barrier, inc=1, device_id={"row": row, "col": column}, device_id_type=MESH
        )

    each(1, n_row, lambda k: greet(on_line(k), col))
    each(1, n_col, lambda k: greet(r, on_plane(k)))

    acc[...] = jnp.zeros_like(acc)
    for load in loads:
        load.wait()
    mine[feats + n_probes :, :] = jnp.concatenate(
        [targets[...], jnp.zeros((rhs_rows - n_probes - 1, width), F32)], 0
    )
    pl.semaphore_wait(barrier, n_row + n_col - 2)

    def copy(src, dst, send, recv, row, column):
        return pltpu.make_async_remote_copy(
            src_ref=src, dst_ref=dst, send_sem=send, recv_sem=recv,
            device_id={"row": row, "col": column}, device_id_type=MESH,
        )

    paired = jnp.minimum(r, n_row - 1 - r)
    low_side = (2 * r < n_row).astype(jnp.int32)

    def order(t):
        near = r + (t % 2) * (-((t + 1) // 2)) + (1 - t % 2) * (t // 2)
        far = low_side * t + (1 - low_side) * (n_row - 1 - t)
        inside = (t <= 2 * paired).astype(jnp.int32)
        return inside * near + (1 - inside) * far

    def block_to(row):
        return copy(mine, held.at[r], line_send.at[row], line_recv.at[r], row, col)

    def block_from(row):
        slot = held.at[row]
        return copy(slot, slot, line_send.at[row], line_recv.at[row], row, col)

    mate = q * 2 + (1 - col % 2)

    def to_mate(row):
        return copy(held.at[row], other.at[row], mate_send.at[row], mate_recv.at[row], r, mate)

    def feats_to(quad):
        return copy(
            mine.at[0:feats], plane.at[q], plane_send.at[quad], plane_recv.at[q],
            r, quad * 2 + col % 2,
        )

    def feats_from(quad):
        slot = plane.at[quad]
        return copy(slot, slot, plane_send.at[quad], plane_recv.at[quad], r, quad * 2 + col % 2)

    def part_to(quad):
        return copy(
            part_out.at[quad], part_in.at[q], part_send.at[quad], part_recv.at[q],
            r, quad * 2 + col % 2,
        )

    def part_from(quad):
        slot = part_in.at[quad]
        return copy(slot, slot, part_send.at[quad], part_recv.at[quad], r, quad * 2 + col % 2)

    def chunk(k):
        if n_quad != 4:
            return (q + k) % n_quad
        x, y = q % 2, q // 2
        return (q, y * 2 + 1 - x, (1 - y) * 2 + x, 3 - q)[k]

    to_mate(r).start()
    block_to(order(1)).start()
    each(1, n_quad, lambda k: feats_to(chunk(k)).start())
    each(2, n_row, lambda t: block_to(order(t)).start())
    plane[q] = mine[0:feats, :]
    inv_two = 0.5 / (ls_ref[0] * ls_ref[0])

    def prepare(k):
        x = plane[chunk(k)]
        lanes_k = pl.ds(pl.multiple_of(k * width, width), width)
        own_sq[:, lanes_k] = jnp.sum(x * x, axis=0, keepdims=True)
        high, middle, low = split_three(x)
        own_split[:, lanes_k] = jnp.concatenate([high, middle, high, low, high, middle], 0)

    def open_pair(row):
        x = jnp.concatenate([held[row, 0:feats, :], other[row, 0:feats, :]], 1)
        x = jnp.transpose(x)
        high, middle, low = split_three(-2.0 * x)
        stack = jnp.concatenate([high, high, middle, high, low, middle], 1)
        sq = jnp.sum(x * x, axis=1, keepdims=True)
        rhs = jnp.concatenate([held[row, feats:, :], other[row, feats:, :]], 1)
        rhs = jnp.concatenate([rhs, jnp.zeros((lhs_rows - rhs_rows, 2 * width), F32)], 0)
        b_high, b_middle, b_low = split_three(rhs)
        return (
            stack,
            sq,
            jnp.concatenate([b_high, b_middle, b_low], 0),
            jnp.concatenate([b_high, b_middle], 0),
        )

    group = 2 if n_quad % 2 == 0 else 1
    span = group * width

    def absorb(opened, index):
        stack, sq, lhs_three, lhs_two = opened
        own = pl.ds(pl.multiple_of(index * span, span), span)
        dots = jnp.dot(stack, own_split[:, own], preferred_element_type=F32)
        dist = jnp.maximum((sq + own_sq[:, own]) + dots, 0.0)
        kern = jnp.exp(dist * (-inv_two))
        both = jnp.concatenate([kern, kern * dist], 1)
        both_high = both.astype(BF16)
        both_middle = (both - both_high.astype(F32)).astype(BF16)
        first = jnp.dot(lhs_three, both_high, preferred_element_type=F32)
        second = jnp.dot(lhs_two, both_middle, preferred_element_type=F32)
        small = (first[2 * lhs_rows :] + second[lhs_rows:]) + (
            first[lhs_rows : 2 * lhs_rows] + second[:lhs_rows]
        )
        acc[index] += first[:lhs_rows] + small

    def send_parts(index, own_too):
        for j in range(group):
            quad = chunk(index * group + j)
            part_out[quad, 0:rhs_rows, :] = acc[index, 0:rhs_rows, j * width : (j + 1) * width]
            part_out[quad, rhs_rows:, :] = acc[
                index, 0:n_probes, span + j * width : span + (j + 1) * width
            ]
            if not (own_too and j == 0):
                part_to(quad).start()

    prepare(0)

    def prepare_other(k):
        feats_from(chunk(k)).wait_recv()
        prepare(k)

    each(1, n_quad, prepare_other)
    n_groups = n_quad // group

    def each_group(first, use):
        if n_groups <= 2:
            for index in range(first, n_groups):
                use(index)
        else:
            pl.loop(first, n_groups)(use)

    for t in range(n_row):
        if t + 1 < n_row:
            block_from(order(t + 1)).wait_recv()
            to_mate(order(t + 1)).start()
        row = order(t)
        arrival = other.at[row]
        copy(arrival, arrival, mate_send.at[row], mate_recv.at[row], r, mate).wait_recv()
        opened = open_pair(row)
        if t < n_row - 1:
            each_group(0, lambda index: absorb(opened, index))
        else:

            def finish(index, own_too=False):
                absorb(opened, index)
                send_parts(index, own_too)

            each_group(1, finish)
            finish(0, True)

    part_in[q] = part_out[q]
    rhs = mine[feats:, :]
    scale = os_ref[0]
    noise = no_ref[0]

    each(1, n_quad, lambda k: part_from(chunk(k)).wait_recv())

    whole = jnp.sum(part_in[...], axis=0)
    eb = whole[0:rhs_rows]
    ed = whole[rhs_rows:]
    kb = scale * eb + noise * rhs
    terms = [rhs * rhs, rhs * kb, kb * kb]
    lanes = up_to(3 * rhs_rows, 128)
    if lanes > 3 * rhs_rows:
        terms.append(jnp.zeros((lanes - 3 * rhs_rows, width), F32))
    row_sums = lax.dot_general(
        jnp.ones((8, width), F32),
        jnp.concatenate(terms, 0),
        NT,
        precision=lax.Precision.HIGHEST,
        preferred_element_type=F32,
    )
    me = r * n_col + col
    n_devices = n_row * n_col
    sums[me] = row_sums[0:1]

    def share(row, column):
        return copy(sums.at[me], sums.at[me], sum_send.at[0], sum_recv.at[0], row, column)

    for dr in range(n_row):
        row = on_line(dr)
        each(1 if dr == 0 else 0, n_col, lambda k: share(row, on_plane(k)).start())

    tall = n_probes + 1
    out_ref[3, 0:n_probes, :] = (scale / (ls_ref[0] * ls_ref[0] * ls_ref[0])) * ed
    out_ref[4, 0:n_probes, :] = eb[0:n_probes]

    shares = sums.at[pl.ds(0, n_devices - 1)]
    all_shares = copy(shares, shares, sum_send.at[0], sum_recv.at[0], r, mate)
    all_shares.wait_recv()
    total = jnp.sum(sums[...], axis=0)
    lane = lax.broadcasted_iota(jnp.int32, (rhs_rows, lanes), 1)
    sub = lax.broadcasted_iota(jnp.int32, (rhs_rows, lanes), 0)

    def column_of(index):
        picked = jnp.where(lane == sub + index * rhs_rows, total, 0.0)
        return jnp.sum(picked, axis=1, keepdims=True)

    norm_old, curv, kb_sq = column_of(0), column_of(1), column_of(2)
    alpha = norm_old / curv
    norm_new = jnp.maximum(alpha * (alpha * kb_sq) - norm_old, 0.0)
    beta = norm_new / norm_old
    residual = rhs - alpha * kb
    for index, value in enumerate((alpha * rhs, residual, residual + beta * rhs)):
        out_ref[index, 0:1, :] = value[n_probes:tall]
        out_ref[index, 1:tall, :] = value[0:n_probes]

    def line_left(k):
        block_to(on_line(k)).wait_send()

    def quad_left(k):
        feats_to(chunk(k)).wait_send()
        part_to(chunk(k)).wait_send()

    each(1, n_row, line_left)
    each(0, n_row, lambda row: to_mate(row).wait_send())
    each(1, n_quad, quad_left)
    all_shares.wait_send()


def unpack(packed, sol_ref, res_ref, dir_ref, len_ref, scl_ref):
    for index, ref in enumerate((sol_ref, res_ref, dir_ref, len_ref, scl_ref)):
        ref[...] = packed[index, 0 : ref.shape[0], :]


def shards(n_row, n_col, points, targets, probes, lengthscale, outputscale, noise):
    feats, width = points.shape
    n_probes = probes.shape[0]
    n_quad = n_col // 2
    rhs_rows = up_to(n_probes + 1, 8)
    lhs_rows = up_to(n_probes + 1, 16)
    rows = feats + rhs_rows
    group = 2 if n_quad % 2 == 0 else 1
    lanes = up_to(3 * rhs_rows, 128)
    vmem = pl.BlockSpec(memory_space=pltpu.VMEM)
    smem = pl.BlockSpec(memory_space=pltpu.SMEM)
    hbm = pl.BlockSpec(memory_space=pltpu.HBM)
    dma = pltpu.SemaphoreType.DMA
    packed = pl.pallas_call(
        functools.partial(kernel, n_row, n_col, feats, n_probes),
        out_shape=jax.ShapeDtypeStruct((5, rhs_rows, width), F32),
        in_specs=[hbm, hbm, hbm, smem, smem, smem],
        out_specs=vmem,
        scratch_shapes=[
            pltpu.VMEM((n_row, rows, width), F32),
            pltpu.VMEM((n_row, rows, width), F32),
            pltpu.VMEM((n_quad, feats, width), F32),
            pltpu.VMEM((1, width), F32),
            pltpu.VMEM((6 * feats, n_quad * width), BF16),
            pltpu.VMEM((1, n_quad * width), F32),
            pltpu.VMEM((n_quad // group, lhs_rows, 2 * group * width), F32),
            pltpu.VMEM((n_quad, rhs_rows + n_probes, width), F32),
            pltpu.VMEM((n_quad, rhs_rows + n_probes, width), F32),
            pltpu.VMEM((n_row * n_col, 1, lanes), F32),
            dma((3,)),
            dma((n_row,)),
            dma((n_row,)),
            dma((n_row,)),
            dma((n_row,)),
            dma((n_quad,)),
            dma((n_quad,)),
            dma((n_quad,)),
            dma((n_quad,)),
            dma((1,)),
            dma((1,)),
        ],
        compiler_params=pltpu.CompilerParams(
            collective_id=0, has_side_effects=True, vmem_limit_bytes=60 << 20
        ),
    )(points, targets[None, :], probes, lengthscale, outputscale, noise)
    tall = jax.ShapeDtypeStruct((n_probes + 1, width), F32)
    short = jax.ShapeDtypeStruct((n_probes, width), F32)
    return pl.pallas_call(
        unpack,
        out_shape=(tall, tall, tall, short, short),
        in_specs=[vmem],
        out_specs=(vmem,) * 5,
    )(packed)


def solution(mesh):
    split = ("row", "col")
    wide = P(None, split)
    return jax.shard_map(
        functools.partial(shards, mesh.shape["row"], mesh.shape["col"]),
        mesh=mesh,
        in_specs=(wide, P(split), wide, P(), P(), P()),
        out_specs=(wide,) * 5,
        check_vma=False,
    )
```

```python
import functools

import jax
import jax.numpy as jnp
from jax import lax
from jax.experimental import pallas as pl
from jax.experimental.pallas import tpu as pltpu
from jax.sharding import PartitionSpec as P

MESH = pl.DeviceIdType.MESH
F32 = jnp.float32
BF16 = jnp.bfloat16
NT = (((1,), (1,)), ((), ()))


def up_to(value, multiple):
    return (value + multiple - 1) // multiple * multiple


def split_three(value):
    high = value.astype(BF16)
    rest = value - high.astype(F32)
    middle = rest.astype(BF16)
    low = (rest - middle.astype(F32)).astype(BF16)
    return high, middle, low


def each(first, last, use):
    if last - first <= 7:
        for k in range(first, last):
            use(k)
    else:
        pl.loop(first, last)(use)


def kernel(
    n_row,
    n_col,
    feats,
    n_probes,
    x_hbm,
    t_hbm,
    p_hbm,
    ls_ref,
    os_ref,
    no_ref,
    out_ref,
    held,
    other,
    plane,
    targets,
    own_split,
    own_sq,
    acc,
    part_out,
    part_in,
    sums,
    load_sem,
    line_send,
    line_recv,
    mate_send,
    mate_recv,
    plane_send,
    plane_recv,
    part_send,
    part_recv,
    sum_send,
    sum_recv,
):
    r = lax.axis_index("row")
    col = lax.axis_index("col")
    n_quad = n_col // 2
    q = col // 2
    width = x_hbm.shape[1]
    rhs_rows = up_to(n_probes + 1, 8)
    lhs_rows = up_to(n_probes + 1, 16)

    mine = held.at[r]
    loads = [
        pltpu.make_async_copy(x_hbm, mine.at[0:feats], load_sem.at[0]),
        pltpu.make_async_copy(p_hbm, mine.at[feats : feats + n_probes], load_sem.at[1]),
        pltpu.make_async_copy(t_hbm, targets, load_sem.at[2]),
    ]
    barrier = pltpu.get_barrier_semaphore()

    def on_line(k):
        return lax.rem(r + k, n_row)

    def on_plane(k):
        return lax.rem(col + k, n_col)

    def greet(row, column):
        pl.semaphore_signal(
            barrier, inc=1, device_id={"row": row, "col": column}, device_id_type=MESH
        )

    each(1, n_row, lambda k: greet(on_line(k), col))
    for load in loads:
        load.start()
    each(1, n_col, lambda k: greet(r, on_plane(k)))

    acc[...] = jnp.zeros_like(acc)
    for load in loads:
        load.wait()
    mine[feats + n_probes :, :] = jnp.concatenate(
        [targets[...], jnp.zeros((rhs_rows - n_probes - 1, width), F32)], 0
    )
    pl.semaphore_wait(barrier, n_row + n_col - 2)

    def copy(src, dst, send, recv, row, column):
        return pltpu.make_async_remote_copy(
            src_ref=src, dst_ref=dst, send_sem=send, recv_sem=recv,
            device_id={"row": row, "col": column}, device_id_type=MESH,
        )

    paired = jnp.minimum(r, n_row - 1 - r)
    low_side = (2 * r < n_row).astype(jnp.int32)

    def order(t):
        near = r + (t % 2) * (-((t + 1) // 2)) + (1 - t % 2) * (t // 2)
        far = low_side * t + (1 - low_side) * (n_row - 1 - t)
        inside = (t <= 2 * paired).astype(jnp.int32)
        return inside * near + (1 - inside) * far

    def block_to(row):
        return copy(mine, held.at[r], line_send.at[row], line_recv.at[r], row, col)

    def block_from(row):
        slot = held.at[row]
        return copy(slot, slot, line_send.at[row], line_recv.at[row], row, col)

    mate = q * 2 + (1 - col % 2)

    def to_mate(row):
        return copy(held.at[row], other.at[row], mate_send.at[row], mate_recv.at[row], r, mate)

    def feats_to(quad):
        return copy(
            mine.at[0:feats], plane.at[q], plane_send.at[quad], plane_recv.at[q],
            r, quad * 2 + col % 2,
        )

    def feats_from(quad):
        slot = plane.at[quad]
        return copy(slot, slot, plane_send.at[quad], plane_recv.at[quad], r, quad * 2 + col % 2)

    def part_to(quad):
        return copy(
            part_out.at[quad], part_in.at[q], part_send.at[quad], part_recv.at[q],
            r, quad * 2 + col % 2,
        )

    def part_from(quad):
        slot = part_in.at[quad]
        return copy(slot, slot, part_send.at[quad], part_recv.at[quad], r, quad * 2 + col % 2)

    def chunk(k):
        if n_quad != 4:
            return (q + k) % n_quad
        x, y = q % 2, q // 2
        return (q, y * 2 + 1 - x, (1 - y) * 2 + x, 3 - q)[k]

    each(1, n_row, lambda t: block_to(order(n_row - t)).start())
    to_mate(r).start()
    each(1, n_quad, lambda k: feats_to(chunk(k)).start())
    plane[q] = mine[0:feats, :]
    inv_two = 0.5 / (ls_ref[0] * ls_ref[0])

    def prepare(k):
        x = jnp.transpose(plane[chunk(k)])
        rows = pl.ds(pl.multiple_of(k * width, width), width)
        own_sq[rows, :] = jnp.broadcast_to(
            jnp.sum(x * x, axis=1, keepdims=True), (width, 2 * width)
        )
        high, middle, low = split_three(-2.0 * x)
        own_split[rows, :] = jnp.concatenate([high, high, middle, high, low, middle], 1)

    def open_pair(row):
        x = jnp.concatenate([held[row, 0:feats, :], other[row, 0:feats, :]], 1)
        high, middle, low = split_three(x)
        stack = jnp.concatenate([high, middle, high, low, high, middle], 0)
        sq = jnp.sum(x * x, axis=0, keepdims=True)
        rhs = jnp.concatenate([held[row, feats:, :], other[row, feats:, :]], 1)
        rhs = jnp.concatenate([rhs, jnp.zeros((lhs_rows - rhs_rows, 2 * width), F32)], 0)
        b_high, b_middle, b_low = split_three(rhs)
        return (
            stack,
            sq,
            jnp.concatenate([b_high, b_middle, b_low], 0),
            jnp.concatenate([b_high, b_middle], 0),
        )

    group = 2 if n_quad % 2 == 0 else 1
    span = group * width

    def absorb(opened, index):
        stack, sq, lhs_three, lhs_two = opened
        rows = pl.ds(pl.multiple_of(index * span, span), span)
        dots = jnp.dot(own_split[rows, :], stack, preferred_element_type=F32)
        dist = jnp.maximum((own_sq[rows, :] + sq) + dots, 0.0)
        kern = jnp.exp(dist * (-inv_two))
        both = jnp.concatenate([kern, kern * dist], 0)
        both_high = both.astype(BF16)
        both_middle = (both - both_high.astype(F32)).astype(BF16)
        first = lax.dot_general(lhs_three, both_high, NT, preferred_element_type=F32)
        second = lax.dot_general(lhs_two, both_middle, NT, preferred_element_type=F32)
        small = (first[2 * lhs_rows :] + second[lhs_rows:]) + (
            first[lhs_rows : 2 * lhs_rows] + second[:lhs_rows]
        )
        acc[index] += first[:lhs_rows] + small

    def send_parts(index, own_too):
        for j in range(group):
            quad = chunk(index * group + j)
            part_out[quad, 0:rhs_rows, :] = acc[index, 0:rhs_rows, j * width : (j + 1) * width]
            part_out[quad, rhs_rows:, :] = acc[
                index, 0:n_probes, span + j * width : span + (j + 1) * width
            ]
            if not (own_too and j == 0):
                part_to(quad).start()

    prepare(0)

    def prepare_other(k):
        feats_from(chunk(k)).wait_recv()
        prepare(k)

    each(1, n_quad, prepare_other)
    n_groups = n_quad // group
    for t in range(n_row):
        if t + 1 < n_row:
            block_from(order(t + 1)).wait_recv()
            to_mate(order(t + 1)).start()
        row = order(t)
        arrival = other.at[row]
        copy(arrival, arrival, mate_send.at[row], mate_recv.at[row], r, mate).wait_recv()
        opened = open_pair(row)
        if t < n_row - 1:
            each(0, n_groups, lambda index: absorb(opened, index))
        else:

            def finish(index, own_too=False):
                absorb(opened, index)
                send_parts(index, own_too)

            each(1, n_groups, finish)
            finish(0, True)

    part_in[q] = part_out[q]
    rhs = mine[feats:, :]
    scale = os_ref[0]
    noise = no_ref[0]

    each(1, n_quad, lambda k: part_from(chunk(k)).wait_recv())

    whole = jnp.sum(part_in[...], axis=0)
    eb = whole[0:rhs_rows]
    ed = whole[rhs_rows:]
    kb = scale * eb + noise * rhs
    terms = [rhs * rhs, rhs * kb, kb * kb]
    lanes = up_to(3 * rhs_rows, 128)
    if lanes > 3 * rhs_rows:
        terms.append(jnp.zeros((lanes - 3 * rhs_rows, width), F32))
    row_sums = lax.dot_general(
        jnp.ones((8, width), F32),
        jnp.concatenate(terms, 0),
        NT,
        precision=lax.Precision.HIGHEST,
        preferred_element_type=F32,
    )
    me = r * n_col + col
    n_devices = n_row * n_col
    sums[me] = row_sums[0:1]

    def share(k):
        peer = lax.rem(me + k, n_devices)
        return copy(
            sums.at[me], sums.at[me], sum_send.at[0], sum_recv.at[0],
            lax.div(peer, n_col), lax.rem(peer, n_col),
        )

    @pl.loop(1, n_devices)
    def _(k):
        share(k).start()

    tall = n_probes + 1
    out_ref[3, 0:n_probes, :] = (scale / (ls_ref[0] * ls_ref[0] * ls_ref[0])) * ed
    out_ref[4, 0:n_probes, :] = eb[0:n_probes]

    shares = sums.at[pl.ds(0, n_devices - 1)]
    all_shares = copy(shares, shares, sum_send.at[0], sum_recv.at[0], r, mate)
    all_shares.wait_recv()
    total = jnp.sum(sums[...], axis=0)
    lane = lax.broadcasted_iota(jnp.int32, (rhs_rows, lanes), 1)
    sub = lax.broadcasted_iota(jnp.int32, (rhs_rows, lanes), 0)

    def column_of(index):
        picked = jnp.where(lane == sub + index * rhs_rows, total, 0.0)
        return jnp.sum(picked, axis=1, keepdims=True)

    norm_old, curv, kb_sq = column_of(0), column_of(1), column_of(2)
    alpha = norm_old / curv
    norm_new = jnp.maximum(alpha * (alpha * kb_sq) - norm_old, 0.0)
    beta = norm_new / norm_old
    residual = rhs - alpha * kb
    for index, value in enumerate((alpha * rhs, residual, residual + beta * rhs)):
        out_ref[index, 0:1, :] = value[n_probes:tall]
        out_ref[index, 1:tall, :] = value[0:n_probes]

    def line_left(k):
        block_to(on_line(k)).wait_send()

    def quad_left(k):
        feats_to(chunk(k)).wait_send()
        part_to(chunk(k)).wait_send()

    each(1, n_row, line_left)
    each(0, n_row, lambda row: to_mate(row).wait_send())
    each(1, n_quad, quad_left)
    all_shares.wait_send()


def unpack(packed, sol_ref, res_ref, dir_ref, len_ref, scl_ref):
    for index, ref in enumerate((sol_ref, res_ref, dir_ref, len_ref, scl_ref)):
        ref[...] = packed[index, 0 : ref.shape[0], :]


def shards(n_row, n_col, points, targets, probes, lengthscale, outputscale, noise):
    feats, width = points.shape
    n_probes = probes.shape[0]
    n_quad = n_col // 2
    rhs_rows = up_to(n_probes + 1, 8)
    lhs_rows = up_to(n_probes + 1, 16)
    rows = feats + rhs_rows
    group = 2 if n_quad % 2 == 0 else 1
    lanes = up_to(3 * rhs_rows, 128)
    vmem = pl.BlockSpec(memory_space=pltpu.VMEM)
    smem = pl.BlockSpec(memory_space=pltpu.SMEM)
    hbm = pl.BlockSpec(memory_space=pltpu.HBM)
    dma = pltpu.SemaphoreType.DMA
    packed = pl.pallas_call(
        functools.partial(kernel, n_row, n_col, feats, n_probes),
        out_shape=jax.ShapeDtypeStruct((5, rhs_rows, width), F32),
        in_specs=[hbm, hbm, hbm, smem, smem, smem],
        out_specs=vmem,
        scratch_shapes=[
            pltpu.VMEM((n_row, rows, width), F32),
            pltpu.VMEM((n_row, rows, width), F32),
            pltpu.VMEM((n_quad, feats, width), F32),
            pltpu.VMEM((1, width), F32),
            pltpu.VMEM((n_quad * width, 6 * feats), BF16),
            pltpu.VMEM((n_quad * width, 2 * width), F32),
            pltpu.VMEM((n_quad // group, lhs_rows, 2 * group * width), F32),
            pltpu.VMEM((n_quad, rhs_rows + n_probes, width), F32),
            pltpu.VMEM((n_quad, rhs_rows + n_probes, width), F32),
            pltpu.VMEM((n_row * n_col, 1, lanes), F32),
            dma((3,)),
            dma((n_row,)),
            dma((n_row,)),
            dma((n_row,)),
            dma((n_row,)),
            dma((n_quad,)),
            dma((n_quad,)),
            dma((n_quad,)),
            dma((n_quad,)),
            dma((1,)),
            dma((1,)),
        ],
        compiler_params=pltpu.CompilerParams(
            collective_id=0, has_side_effects=True, vmem_limit_bytes=60 << 20
        ),
    )(points, targets[None, :], probes, lengthscale, outputscale, noise)
    tall = jax.ShapeDtypeStruct((n_probes + 1, width), F32)
    short = jax.ShapeDtypeStruct((n_probes, width), F32)
    return pl.pallas_call(
        unpack,
        out_shape=(tall, tall, tall, short, short),
        in_specs=[vmem],
        out_specs=(vmem,) * 5,
    )(packed)


def solution(mesh):
    split = ("row", "col")
    wide = P(None, split)
    return jax.shard_map(
        functools.partial(shards, mesh.shape["row"], mesh.shape["col"]),
        mesh=mesh,
        in_specs=(wide, P(split), wide, P(), P(), P()),
        out_specs=(wide,) * 5,
        check_vma=False,
    )
```
